256 devices in a mesh: table: 64 (over y, z, core), dp: 4 (over x).
Axes of the slice: x: 4, y: 4, z: 8, core: 2. Of those that a mesh axis runs over, the one named last changes fastest.
Arguments:
- owners: int32 [131072, 8], P(('table', 'dp')), may hold values from 0 to 63, all different within a row; in each aligned block of 512 rows (0 to 511, 512 to 1023, ...) at most 128 rows name the same one
- local_rows: int32 [131072, 8], P(('table', 'dp')), may hold values from 0 to 4095
- grad_pooled: bfloat16 [131072, 128], P(('table', 'dp')), may hold values from -4 to 4
- table: float32 [262144, 128], P('table'), may hold values from -6 to 6
- accum: float32 [262144], P('table'), may hold values from 0.1 to 4
- parity: float32 [8192, 128], P('table'), may hold values from -6 to 6
- parity_slot: int32 [262144], P('table'), may hold values from 0 to 8191, as said below
Outputs:
- pooled: bfloat16 [131072, 128], P(('table', 'dp'))
- new_table: float32 [262144, 128], P('table')
- new_accum: float32 [262144], P('table')
- new_parity: float32 [8192, 128], P('table')
The draws below stay inside these ranges and needn't reach their ends.
Inputs may be any that keep to these rules, and one draw needn't show every extreme that they name: `owners`: each bag names 8 different table devices. Among the 512 bags of one device (aligned blocks of rows), no table device is named by more than 128 bags, and in some blocks one is named by exactly 128. `parity_slot`: within the 4096 rows of one table device the values are distinct, and each device's rows include the value 8192 - 1. Parity row v is held by the table device v // 128.
All inputs are finite; a program needn't handle non-finite values.
Results may differ from the reference program's by a relative error of at most 0.0085.
Values may be sent and summed in bfloat16 or wider, within the bound.
A program may use at most 64 MiB of HBM per device.

```python
import math
import jax
import jax.numpy as jnp
import numpy as np
from jax import lax

E = 128
HOT = 8
B_DEV = 512
R_DEV = 4096
CAP = 128
PSLOTS = 8192
ROWS = 262144
BAGS = 131072
N_TABLE = 64


def draw_parity_slot(key, part):
    device_keys = jax.random.split(key, ROWS // R_DEV)

    def one_device(device_key):
        chosen = jax.random.permutation(device_key, PSLOTS)[:R_DEV]
        present = jnp.any(chosen == PSLOTS - 1)
        return chosen.at[0].set(jnp.where(present, chosen[0], PSLOTS - 1))
    return jax.vmap(one_device)(device_keys).reshape(ROWS).astype(jnp.int32)


def touch_ends(result, key, smallest, high):
    longest = result.shape.index(max(result.shape))
    spots = []
    for shift in (0, 1):
        where = [jax.random.randint(jax.random.fold_in(key, axis), (), 0, length) for axis, length in enumerate(result.shape)]
        where[longest] = (where[longest] + shift) % result.shape[longest]
        spots.append(tuple(where))
    return result.at[spots[0]].set(smallest).at[spots[1]].set(high)


def steps_of(key, extent, shards, least, top_value):
    def one(dim, shards_of):
        draws = jax.random.uniform(jax.random.fold_in(jax.random.fold_in(key, 6), dim), (shards_of,), jnp.float32, least / len(shards), top_value / len(shards))
        return jnp.repeat(jnp.exp(draws), extent[dim] // shards_of).reshape((-1,) + (1,) * (len(extent) - dim - 1))

    level = one(*shards[0])
    for cut in shards[1:]:
        level = level * one(*cut)
    return level


def assign_block(rng, own, number, rows, count, top, bound, slope):
    ranking = jax.random.permutation(rng, count)
    heavy_load, ordinary = shares(count, rows * top, bound, slope, True), shares(count, rows * top, bound, slope, False)
    places = jnp.arange(count)

    def named(tallies, offset_by):
        used = int((tallies > 0).sum())
        fixed = max(1, used // 4)
        shifted = fixed + (places - fixed + offset_by * (used - fixed)) % max(1, count - fixed)
        return jnp.zeros((count,), jnp.int32).at[ranking[jnp.where(places < fixed, places, shifted)]].set(jnp.asarray(tallies, jnp.int32))

    tallies = jnp.where(number % 4 == 0, named(heavy_load, number // 4), named(ordinary, number - number // 4 - 1))
    mixed = jax.random.permutation(jax.random.fold_in(own, 3), count)
    giver, receiver = mixed[0:count // 2 * 2:2], mixed[1:count // 2 * 2:2]
    margin = jnp.minimum(tallies[giver] - 1, bound - tallies[receiver]) // 2
    margin = jnp.where((giver == ranking[0]) | (receiver == ranking[0]) | (tallies[receiver] == 0), 0, jnp.maximum(margin, 0))
    shifted = jax.random.randint(jax.random.fold_in(own, 4), (count // 2,), 0, 1 << 20) % (margin + 1)
    tallies = tallies.at[giver].add(-shifted).at[receiver].add(shifted)
    labels = jnp.searchsorted(jnp.cumsum(tallies), jnp.arange(rows * top), side="right").astype(jnp.int32)
    listing = labels.reshape(top, rows).T
    listing = listing[jax.random.permutation(jax.random.fold_in(own, 1), rows)]
    offset_by = jax.random.randint(jax.random.fold_in(own, 2), (rows, 1), 0, top)
    return jnp.take_along_axis(listing, (jnp.arange(top)[None, :] + offset_by) % top, axis=1)


def shares(amount, total, most, lean, full):
    weights = [(1 << 20) // math.isqrt(grade ** lean) + 1 for grade in range(1, amount + 1)]
    largest = most if full else min(most, max(-(-total // amount), total * weights[0] // sum(weights)))
    least = 1 if total - largest >= amount - 1 else 0
    given, surplus = [largest] + [least] * (amount - 1), total - largest - least * (amount - 1)
    while surplus > 0:
        free = [i for i in range(1, amount) if given[i] < largest] or [i for i in range(1, amount) if given[i] < most]
        pool, left = sum([weights[i] for i in free]), surplus
        for i in free:
            extra = min(most - given[i], max(1, left * weights[i] // pool), surplus)
            given[i] = given[i] + extra
            surplus = surplus - extra
    return np.array(given)


def noise(key, shape, scale, most, cuts=(), dtype=jnp.bfloat16):
    factor_of = steps_of(key, shape, cuts, -0.22, 0.18) if cuts else 1.0
    result = jax.random.normal(key, shape, jnp.float32) * scale * factor_of
    return jnp.minimum(jnp.maximum(result, -most), most).astype(dtype)


def setup_inputs(seed: int = 0) -> dict:
    key_list = jax.random.split(jax.random.key(seed), 8)
    owners_keys = jax.random.split(jax.random.fold_in(key_list[0], 1), BAGS // B_DEV)
    owners_turns = jax.random.permutation(jax.random.fold_in(key_list[0], 3), BAGS // B_DEV)
    owners = jax.vmap(lambda own, number: assign_block(jax.random.fold_in(key_list[0], 2), own, number, B_DEV, N_TABLE, HOT, CAP, 1))(owners_keys, owners_turns).reshape((BAGS, HOT))
    local_rows = touch_ends(jax.random.randint(key_list[1], (BAGS, HOT), 0, R_DEV), jax.random.fold_in(key_list[1], 1), 0, R_DEV - 1).astype(jnp.int32)
    grad_pooled = noise(key_list[2], (BAGS, E), 0.5, 4.0, ((0, 256),))
    table = noise(key_list[3], (ROWS, E), 1.0, 6.0, ((0, 64),), jnp.float32)
    accum = jnp.clip(jnp.exp(math.log(4.0) - 3.6888794 * jax.random.uniform(key_list[4], (ROWS,), jnp.float32) ** steps_of(key_list[4], (ROWS,), ((0, 64),), -0.2, 0.2)), 0.1, 4.0)
    parity = noise(key_list[5], (PSLOTS, E), 1.0, 6.0, ((0, 64),), jnp.float32)
    parity_slot = draw_parity_slot(jax.random.fold_in(key_list[7], 71), 0)
    return {"owners": owners, "local_rows": local_rows, "grad_pooled": grad_pooled, "table": table, "accum": accum, "parity": parity, "parity_slot": parity_slot}


LEARN = 0.5
EPSILON = 1e-06

def reference(owners, local_rows, grad_pooled, table, accum, parity, parity_slot):
    row_index = (owners * R_DEV + local_rows).astype(jnp.int32)
    table_half = table.astype(jnp.bfloat16)
    pooled = jnp.zeros((BAGS, E), jnp.float32)
    row_grads = jnp.zeros((ROWS, E), jnp.float32)
    bag_grads = grad_pooled.astype(jnp.float32)
    for lookup in range(HOT):
        pooled = pooled + table_half[row_index[:, lookup]].astype(jnp.float32)
        row_grads = row_grads.at[row_index[:, lookup]].add(bag_grads)
    new_accum = accum + lax.optimization_barrier(jnp.mean(row_grads * row_grads, axis=1))
    new_table = table - LEARN * row_grads / jnp.sqrt(new_accum + EPSILON)[:, None]
    row_delta = new_table - table
    new_parity = parity + jax.ops.segment_sum(row_delta, parity_slot, num_segments=PSLOTS)
    return (pooled.astype(jnp.bfloat16), new_table, new_accum, new_parity)
```

```python
import functools

import jax
import jax.numpy as jnp
from jax import lax
from jax.experimental import pallas as pl
from jax.experimental.pallas import tpu as pltpu
from jax.sharding import PartitionSpec as P

LEARN = 0.5
EPSILON = 1e-06
F32, BF16, I32 = jnp.float32, jnp.bfloat16, jnp.int32
VMEM = pl.BlockSpec(memory_space=pltpu.VMEM)
SMEM = pl.BlockSpec(memory_space=pltpu.SMEM)
PARAMS = pltpu.CompilerParams(vmem_limit_bytes=48 * 1024 * 1024)


def pack_kernel(rank_ref, grads_ref, rows_ref, out_ref, req_ref):
    owners, bags = rank_ref.shape
    slots = out_ref.shape[1]
    grads = grads_ref[...]
    slot = lax.broadcasted_iota(I32, (slots, bags), 0)

    def one(o, carry):
        hot = slot == rank_ref[pl.ds(o, 1), :]
        out_ref[o] = jnp.dot(
            hot.astype(F32).astype(BF16), grads, preferred_element_type=F32
        ).astype(BF16)
        code = jnp.where(hot, rows_ref[pl.ds(o, 1), :] + 1, 0)
        req_ref[pl.ds(o, 1), :] = jnp.sum(code.T, axis=0, keepdims=True) - 1
        return carry

    lax.fori_loop(0, owners, one, 0)


def pick_kernel(req_ref, table_ref, out_ref, line):
    sources, slots = req_ref.shape

    def one(p, carry):
        for s in range(slots):
            line[pl.ds(s, 1), :] = table_ref[pl.ds(req_ref[p, s], 1), :]
        out_ref[p] = line[...].astype(BF16)
        return carry

    lax.fori_loop(0, sources, one, 0)


def pool_kernel(rank_ref, rows_ref, out_ref, total):
    owners, bags = rank_ref.shape
    slots = rows_ref.shape[1]
    slot = lax.broadcasted_iota(I32, (slots, bags), 0)
    total[...] = jnp.zeros_like(total)

    def one(i, carry):
        hot = jnp.concatenate(
            [slot == rank_ref[pl.ds(2 * i, 1), :], slot == rank_ref[pl.ds(2 * i + 1, 1), :]], axis=0
        )
        rows = jnp.concatenate([rows_ref[2 * i], rows_ref[2 * i + 1]], axis=0)
        total[...] += lax.dot_general(
            rows, hot.astype(F32).astype(BF16), (((0,), (0,)), ((), ())), preferred_element_type=F32
        )
        return carry

    lax.fori_loop(0, owners // 2, one, 0)
    out_ref[...] = total[...].T.astype(BF16)


def add_kernel(req_ref, grads_ref, out_ref, total, chunk=512, group=4):
    sources, slots = req_ref.shape
    rows = total.shape[0]
    total[...] = jnp.zeros_like(total)
    row = lax.broadcasted_iota(I32, (chunk, slots), 0)

    def one(i, carry):
        lines = [req_ref[pl.ds(group * i + k, 1), :] for k in range(group)]
        grads = jnp.concatenate([grads_ref[group * i + k] for k in range(group)], axis=0)
        for c in range(0, rows, chunk):
            hot = jnp.concatenate([row == line - c for line in lines], axis=1)
            total[c : c + chunk, :] += jnp.dot(
                hot.astype(F32).astype(BF16), grads, preferred_element_type=F32
            )
        return carry

    lax.fori_loop(0, sources // group, one, 0)
    out_ref[...] = total[...].astype(BF16)


def place_kernel(code_ref, delta_ref, out_ref, chunk=512):
    count = out_ref.shape[0]
    lines, lanes = code_ref.shape
    slot = lax.broadcasted_iota(I32, (chunk, lanes), 0)
    delta = delta_ref[...]

    def one(i, carry):
        base = pl.multiple_of(i * chunk, chunk)
        hot = jnp.concatenate(
            [slot == code_ref[k : k + 1, :] - base for k in range(lines)], axis=1
        )
        out_ref[pl.ds(base, chunk), :] = jnp.dot(
            hot.astype(F32).astype(BF16), delta, preferred_element_type=F32
        ).astype(BF16)
        return carry

    lax.fori_loop(0, count // chunk, one, 0)


def on_device(owners, local_rows, grad_pooled, table, accum, parity, parity_slot):
    table_count, dp_count = lax.axis_size("table"), lax.axis_size("dp")
    bags, hot = owners.shape
    rows, width = table.shape
    cap = min(bags, 2 * bags * hot // table_count)
    mine = lax.axis_index("dp")

    named = owners.T[:, None, :] == jnp.arange(table_count, dtype=I32)[None, :, None]
    hits = jnp.any(named, axis=0)
    wanted = jnp.sum(jnp.where(named, local_rows.T[:, None, :], 0), axis=0)
    before = jnp.arange(bags)[:, None] < jnp.arange(bags)[None, :]
    rank = jnp.dot(hits.astype(BF16), before.astype(BF16), preferred_element_type=F32)
    rank = jnp.where(hits, rank.astype(I32), -1)

    outgoing, requests = pl.pallas_call(
        pack_kernel,
        out_shape=(
            jax.ShapeDtypeStruct((table_count, cap, width), BF16),
            jax.ShapeDtypeStruct((table_count, cap), I32),
        ),
        in_specs=[VMEM] * 3,
        out_specs=(VMEM, VMEM),
        compiler_params=PARAMS,
        name="pack",
    )(rank, grad_pooled, wanted)
    exchange = functools.partial(
        lax.all_to_all, axis_name="table", split_axis=0, concat_axis=0, tiled=True
    )
    asked = exchange(requests)
    incoming = exchange(outgoing)
    fetched = pl.pallas_call(
        pick_kernel,
        out_shape=jax.ShapeDtypeStruct((table_count, cap, width), BF16),
        in_specs=[SMEM, VMEM],
        out_specs=VMEM,
        scratch_shapes=[pltpu.VMEM((cap, width), F32)],
        compiler_params=PARAMS,
        name="pick",
    )(jnp.maximum(asked, 0), table)
    returned = exchange(fetched)
    partial_grads = pl.pallas_call(
        add_kernel,
        out_shape=jax.ShapeDtypeStruct((rows, width), BF16),
        in_specs=[VMEM] * 2,
        out_specs=VMEM,
        scratch_shapes=[pltpu.VMEM((rows, width), F32)],
        compiler_params=PARAMS,
        name="add",
    )(asked, incoming)
    quarters = lax.all_to_all(
        partial_grads.reshape(dp_count, rows // dp_count, width), "dp", 0, 0, tiled=True
    )
    quarter = jnp.sum(quarters.astype(F32), axis=0).astype(BF16)
    row_grads = lax.all_gather(quarter, "dp", axis=0, tiled=True).astype(F32)
    new_accum = accum + jnp.mean(row_grads * row_grads, axis=1)
    new_table = table - LEARN * row_grads / jnp.sqrt(new_accum + EPSILON)[:, None]
    row_delta = new_table - table

    parity_count = parity.shape[0]
    part = parity_count // dp_count
    holder, place = parity_slot // parity_count, parity_slot % parity_count
    code = jnp.where(place // part == mine, holder * part + place % part, -1)
    spread = pl.pallas_call(
        place_kernel,
        out_shape=jax.ShapeDtypeStruct((table_count * part, width), BF16),
        in_specs=[VMEM] * 2,
        out_specs=VMEM,
        compiler_params=PARAMS,
        name="place",
    )(code.reshape(rows // 128, 128), row_delta.astype(BF16))
    arrived = exchange(spread.reshape(table_count, part, width))
    part_sum = jnp.sum(arrived.astype(F32), axis=0)
    new_parity = parity + lax.all_gather(part_sum, "dp", axis=0, tiled=True)
    pooled = pl.pallas_call(
        pool_kernel,
        out_shape=jax.ShapeDtypeStruct((bags, width), BF16),
        in_specs=[VMEM] * 2,
        out_specs=VMEM,
        scratch_shapes=[pltpu.VMEM((width, bags), F32)],
        compiler_params=PARAMS,
        name="pool",
    )(rank, returned)
    return (pooled, new_table, new_accum, new_parity)


def solution(mesh):
    in_specs = (
        P(("table", "dp"), None),
        P(("table", "dp"), None),
        P(("table", "dp"), None),
        P("table", None),
        P("table"),
        P("table", None),
        P("table"),
    )
    out_specs = (P(("table", "dp"), None), P("table", None), P("table"), P("table", None))
    return jax.shard_map(
        on_device, mesh=mesh, in_specs=in_specs, out_specs=out_specs, check_vma=False
    )
```

```python
import functools

import jax
import jax.numpy as jnp
from jax import lax
from jax.experimental import pallas as pl
from jax.experimental.pallas import tpu as pltpu
from jax.sharding import PartitionSpec as P

LEARN = 0.5
EPSILON = 1e-06
F32, BF16, I32 = jnp.float32, jnp.bfloat16, jnp.int32
VMEM = pl.BlockSpec(memory_space=pltpu.VMEM)
MESH = pl.DeviceIdType.MESH
PARAMS = pltpu.CompilerParams(vmem_limit_bytes=48 * 1024 * 1024)


def front_kernel(
    rank_ref, grads_ref, wanted_ref, table_ref, pooled_ref, sums_ref,
    table, g_out, g_in, q_out, q_in, q_line, q_smem, r_out, r_in, total, pool, part, quarter_in,
    line, gs, gr, qs, qr, rs, rr, ps, pr, us, ur, table_sem, q_sem,
):
    n, bags = rank_ref.shape
    slots, width = g_out.shape[1:]
    rows = total.shape[0]
    dp = quarter_in.shape[0]
    quarter = rows // dp
    me, mine = lax.axis_index("table"), lax.axis_index("dp")

    def offset(k):
        j = (k + 1) // 2
        return (k % 2) * j + (1 - k % 2) * (n - j)

    def to(k):
        return (me + offset(k)) % n

    def frm(k):
        return (me + n - offset(k)) % n

    def copy(out, into, send, recv, peer, place):
        return pltpu.make_async_remote_copy(
            src_ref=out.at[peer], dst_ref=into.at[place], send_sem=send.at[peer],
            recv_sem=recv.at[place], device_id={"table": peer}, device_id_type=MESH,
        )

    def dp_to(k):
        return (mine + k) % dp

    def quarter_of(d):
        return pl.ds(pl.multiple_of(d * quarter, quarter), quarter)

    def reduce_copy(peer, place):
        return pltpu.make_async_remote_copy(
            src_ref=part.at[quarter_of(peer)], dst_ref=quarter_in.at[place], send_sem=ps.at[peer],
            recv_sem=pr.at[place], device_id={"dp": peer}, device_id_type=MESH,
        )

    def gather_copy(peer, place):
        return pltpu.make_async_remote_copy(
            src_ref=sums_ref.at[quarter_of(place)], dst_ref=sums_ref.at[quarter_of(place)],
            send_sem=us.at[peer], recv_sem=ur.at[place], device_id={"dp": peer},
            device_id_type=MESH,
        )

    barrier = pltpu.get_barrier_semaphore()

    def greet(k, carry):
        pl.semaphore_signal(barrier, inc=1, device_id={"table": (me + k) % n}, device_id_type=MESH)
        return carry

    lax.fori_loop(1, n, greet, 0)
    for k in range(1, dp):
        pl.semaphore_signal(barrier, inc=1, device_id={"dp": dp_to(k)}, device_id_type=MESH)
    load = pltpu.make_async_copy(table_ref, table.at[0:rows], table_sem)
    load.start()
    table[rows : rows + 8, :] = jnp.zeros((8, width), F32)
    pl.semaphore_wait(barrier, n - 1 + dp - 1)

    slot = lax.broadcasted_iota(I32, (slots, bags), 0)

    def packed(o):
        hot = slot == rank_ref[pl.ds(o, 1), :]
        lines = jnp.dot(hot.astype(F32).astype(BF16), grads_ref[...], preferred_element_type=F32)
        code = jnp.where(hot, wanted_ref[pl.ds(o, 1), :] + 1, 0)
        code = sum(code[:, c : c + slots] for c in range(0, bags, slots))
        code = jnp.sum(code.T, axis=0, keepdims=True)
        code = jnp.where(code == 0, rows, code - 1)
        return lines.astype(BF16), jnp.broadcast_to(code, (8, slots))

    def pack(k, carry):
        o = to(k)
        lines, code = packed(o)
        q_out[o] = code
        copy(q_out, q_in, qs, qr, o, me).start()
        g_out[o] = lines
        copy(g_out, g_in, gs, gr, o, me).start()
        return carry

    lax.fori_loop(1, n, pack, 0)
    lines, code = packed(me)
    g_in[me] = lines
    q_in[me] = code

    def asked(k, carry):
        p = frm(k)
        copy(q_out, q_in, qs, qr, p, p).wait_recv()
        return carry

    lax.fori_loop(1, n, asked, 0)
    for p in range(n):
        q_line[p : p + 1, :] = q_in[p, 0:1, :]
    fetch = pltpu.make_async_copy(q_line, q_smem, q_sem)
    fetch.start()
    fetch.wait()
    load.wait()

    def pick(p):
        for s in range(slots):
            line[pl.ds(s, 1), :] = table[pl.ds(q_smem[p, s], 1), :]
        return line[...].astype(BF16)

    def serve(k, carry):
        p = frm(k)
        r_out[p] = pick(p)
        copy(r_out, r_in, rs, rr, p, me).start()
        return carry

    lax.fori_loop(1, n, serve, 0)
    r_in[me] = pick(me)

    total[...] = jnp.zeros_like(total)
    chunk, group = 512, 4
    row = lax.broadcasted_iota(I32, (chunk, slots), 0)

    def add(i, carry):
        sources = [frm(group * i + j) for j in range(group)]
        for j, p in enumerate(sources):

            def arrive(p=p):
                copy(g_out, g_in, gs, gr, p, p).wait_recv()

            if j == 0:
                pl.when(i > 0)(arrive)
            else:
                arrive()
        lines = [q_line[pl.ds(p, 1), :] for p in sources]
        grads = jnp.concatenate([g_in[p] for p in sources], axis=0)
        for c in range(0, rows, chunk):
            hot = jnp.concatenate([row == one - c for one in lines], axis=1)
            total[c : c + chunk, :] += jnp.dot(
                hot.astype(F32).astype(BF16), grads, preferred_element_type=F32
            )
        return carry

    lax.fori_loop(0, n // group, add, 0)
    part[...] = total[...].astype(BF16)
    for k in range(1, dp):
        reduce_copy(dp_to(k), mine).start()
    summed = total[quarter_of(mine), :].astype(BF16).astype(F32)
    for k in range(1, dp):
        d = dp_to(k)
        reduce_copy(d, d).wait_recv()
        summed = summed + quarter_in[d].astype(F32)
    sums_ref[quarter_of(mine), :] = summed.astype(BF16)
    for k in range(1, dp):
        gather_copy(dp_to(k), mine).start()

    pool[...] = jnp.zeros_like(pool)

    def gather(i, carry):
        sources = [frm(2 * i), frm(2 * i + 1)]

        @pl.when(i > 0)
        def _():
            copy(r_out, r_in, rs, rr, sources[0], sources[0]).wait_recv()

        copy(r_out, r_in, rs, rr, sources[1], sources[1]).wait_recv()
        hot = jnp.concatenate([slot == rank_ref[pl.ds(o, 1), :] for o in sources], axis=0)
        lines = jnp.concatenate([r_in[o] for o in sources], axis=0)
        pool[...] += lax.dot_general(
            lines, hot.astype(F32).astype(BF16), (((0,), (0,)), ((), ())),
            preferred_element_type=F32,
        )
        return carry

    lax.fori_loop(0, n // 2, gather, 0)
    pooled_ref[...] = pool[...].T.astype(BF16)

    def sent(k, carry):
        p = to(k)
        copy(q_out, q_in, qs, qr, p, me).wait_send()
        copy(g_out, g_in, gs, gr, p, me).wait_send()
        copy(r_out, r_in, rs, rr, p, me).wait_send()
        return carry

    lax.fori_loop(1, n, sent, 0)
    for k in range(1, dp):
        d = dp_to(k)
        reduce_copy(d, mine).wait_send()
        gather_copy(d, d).wait_recv()
        gather_copy(d, mine).wait_send()


def front(rank, grads, wanted, table, dp):
    n, bags = rank.shape
    rows, width = table.shape
    cap = min(bags, 128)
    dma = pltpu.SemaphoreType.DMA
    blocks = pltpu.VMEM((n, cap, width), BF16)
    return pl.pallas_call(
        front_kernel,
        out_shape=(
            jax.ShapeDtypeStruct((bags, width), BF16),
            jax.ShapeDtypeStruct((rows, width), BF16),
        ),
        in_specs=[VMEM, VMEM, VMEM, pl.BlockSpec(memory_space=pl.ANY)],
        out_specs=(VMEM, VMEM),
        scratch_shapes=[
            pltpu.VMEM((rows + 8, width), F32),
            blocks,
            blocks,
            pltpu.VMEM((n, 8, cap), I32),
            pltpu.VMEM((n, 8, cap), I32),
            pltpu.VMEM((n, cap), I32),
            pltpu.SMEM((n, cap), I32),
            blocks,
            blocks,
            pltpu.VMEM((rows, width), F32),
            pltpu.VMEM((width, bags), F32),
            pltpu.VMEM((rows, width), BF16),
            pltpu.VMEM((dp, rows // dp, width), BF16),
            pltpu.VMEM((cap, width), F32),
        ]
        + [dma((n,))] * 6
        + [dma((dp,))] * 4
        + [dma, dma],
        compiler_params=pltpu.CompilerParams(
            vmem_limit_bytes=48 * 1024 * 1024, collective_id=0, has_side_effects=True
        ),
        name="front",
    )(rank, grads, wanted, table)


def place_kernel(code_ref, delta_ref, out_ref, chunk=512):
    count = out_ref.shape[0]
    lines, lanes = code_ref.shape
    slot = lax.broadcasted_iota(I32, (chunk, lanes), 0)
    delta = delta_ref[...]

    def one(i, carry):
        base = pl.multiple_of(i * chunk, chunk)
        hot = jnp.concatenate(
            [slot == code_ref[k : k + 1, :] - base for k in range(lines)], axis=1
        )
        out_ref[pl.ds(base, chunk), :] = jnp.dot(
            hot.astype(F32).astype(BF16), delta, preferred_element_type=F32
        ).astype(BF16)
        return carry

    lax.fori_loop(0, count // chunk, one, 0)


def on_device(owners, local_rows, grad_pooled, table, accum, parity, parity_slot):
    table_count, dp_count = lax.axis_size("table"), lax.axis_size("dp")
    bags, hot = owners.shape
    rows, width = table.shape
    mine = lax.axis_index("dp")

    named = owners.T[:, None, :] == jnp.arange(table_count, dtype=I32)[None, :, None]
    hits = jnp.any(named, axis=0)
    wanted = jnp.sum(jnp.where(named, local_rows.T[:, None, :], 0), axis=0)
    before = jnp.arange(bags)[:, None] < jnp.arange(bags)[None, :]
    rank = jnp.dot(hits.astype(BF16), before.astype(BF16), preferred_element_type=F32)
    rank = jnp.where(hits, rank.astype(I32), -1)

    pooled, sums = front(rank, grad_pooled, wanted, table, dp_count)
    row_grads = sums.astype(F32)
    exchange = functools.partial(
        lax.all_to_all, axis_name="table", split_axis=0, concat_axis=0, tiled=True
    )
    new_accum = accum + jnp.mean(row_grads * row_grads, axis=1)
    new_table = table - LEARN * row_grads / jnp.sqrt(new_accum + EPSILON)[:, None]
    row_delta = new_table - table

    parity_count = parity.shape[0]
    part = parity_count // dp_count
    holder, place = parity_slot // parity_count, parity_slot % parity_count
    code = jnp.where(place // part == mine, holder * part + place % part, -1)
    spread = pl.pallas_call(
        place_kernel,
        out_shape=jax.ShapeDtypeStruct((table_count * part, width), BF16),
        in_specs=[VMEM] * 2,
        out_specs=VMEM,
        compiler_params=PARAMS,
        name="place",
    )(code.reshape(rows // 128, 128), row_delta.astype(BF16))
    arrived = exchange(spread.reshape(table_count, part, width))
    part_sum = jnp.sum(arrived.astype(F32), axis=0)
    new_parity = parity + lax.all_gather(part_sum, "dp", axis=0, tiled=True)
    return (pooled, new_table, new_accum, new_parity)


def solution(mesh):
    in_specs = (
        P(("table", "dp"), None),
        P(("table", "dp"), None),
        P(("table", "dp"), None),
        P("table", None),
        P("table"),
        P("table", None),
        P("table"),
    )
    out_specs = (P(("table", "dp"), None), P("table", None), P("table"), P("table", None))
    return jax.shard_map(
        on_device, mesh=mesh, in_specs=in_specs, out_specs=out_specs, check_vma=False
    )
```

```python
import jax
import jax.numpy as jnp
from jax import lax
from jax.experimental import pallas as pl
from jax.experimental.pallas import tpu as pltpu
from jax.sharding import PartitionSpec as P

LEARN = 0.5
EPSILON = 1e-06
F32, BF16, I32 = jnp.float32, jnp.bfloat16, jnp.int32
VMEM = pl.BlockSpec(memory_space=pltpu.VMEM)
MESH = pl.DeviceIdType.MESH
NY, NZ, NC = 4, 8, 2
NQ = NY * NC
CAP = 128
HALVES = 2


def near(k):
    j = (k + 1) // 2
    return (k % 2) * j + (1 - k % 2) * ((NZ - j) % NZ)


def step_kernel(
    code_ref, grads_ref, table_ref, accum_ref, slot_ref, parity_ref,
    pooled_ref, new_table_ref, new_accum_ref, new_parity_ref,
    table, wide_accum, line_in, code_in, marks, g_out, g_in, q_out, q_in, q_smem, r_out, r_in,
    total, part, quarter_in, sums, pool_out, pool_in, line, placed, core_out, core_in,
    z_out, z_in, y_out, y_in, x_part,
    code_s, code_r, line_s, line_r, g_s, g_r, q_s, q_r, r_s, r_r, part_s, part_r, sum_s, sum_r,
    pool_s, pool_r, core_s, core_r, z_s, z_r, y_s, y_r, x_s, x_r, table_sem, smem_sem,
):
    bags = code_ref.shape[2]
    rows, width = table_ref.shape
    dp = sums.shape[0]
    quarter = rows // dp
    half = quarter // HALVES
    me, mine = lax.axis_index("table"), lax.axis_index("dp")
    z, c, y = (me // NC) % NZ, me % NC, me // (NC * NZ)
    q = y * NC + c

    def remote(src, dst, send, recv, **where):
        return pltpu.make_async_remote_copy(
            src_ref=src, dst_ref=dst, send_sem=send, recv_sem=recv, device_id=where,
            device_id_type=MESH,
        )

    def on_line(other):
        return (me - z * NC) + other * NC

    def on_plane(other):
        return (other // NC) * (NZ * NC) + z * NC + other % NC

    def code_copy(peer, place):
        return remote(code_ref.at[peer], code_in.at[place], code_s.at[peer], code_r.at[place],
                      table=on_line(peer))

    def line_copy(peer, place):
        return remote(grads_ref, line_in.at[place], line_s.at[peer], line_r.at[place],
                      table=on_line(peer))

    def g_copy(peer, place, s):
        return remote(g_out.at[peer, s], g_in.at[place, s], g_s.at[peer, s], g_r.at[place, s],
                      table=on_plane(peer))

    def q_rows(o):
        return pl.ds(pl.multiple_of(o * NZ, NZ), NZ)

    def q_copy(peer, place):
        return remote(q_out.at[q_rows(peer)], q_in.at[q_rows(place)], q_s.at[peer], q_r.at[place],
                      table=on_plane(peer))

    def r_rows(o):
        return pl.ds(pl.multiple_of(o * CAP, CAP), CAP)

    def r_copy(peer, place, s):
        return remote(r_out.at[peer, s], r_in.at[s, r_rows(place)], r_s.at[peer, s],
                      r_r.at[place, s], table=on_plane(peer))

    def half_rows(h):
        return pl.ds(h * half, half)

    def part_copy(peer, place, h):
        return remote(part.at[peer, half_rows(h)], quarter_in.at[place, half_rows(h)],
                      part_s.at[peer, h], part_r.at[place, h], dp=peer)

    def sum_copy(peer, place, h):
        return remote(sums.at[place, half_rows(h)], sums.at[place, half_rows(h)],
                      sum_s.at[peer, h], sum_r.at[place, h], dp=peer)

    def pool_copy(peer, place):
        return remote(pool_out.at[peer], pool_in.at[place], pool_s.at[peer], pool_r.at[place],
                      table=on_line(peer))

    def core_copy():
        return remote(core_out, core_in, core_s, core_r, table=me + 1 - 2 * c)

    def z_copy(peer, place):
        return remote(z_out.at[peer], z_in.at[place], z_s.at[peer], z_r.at[place],
                      table=on_line(peer))

    def y_copy(peer, place):
        return remote(y_out.at[peer], y_in.at[place], y_s.at[peer], y_r.at[place],
                      table=on_plane(peer * NC + c))

    def x_copy(peer, place):
        return remote(x_part.at[place], x_part.at[place], x_s.at[peer], x_r.at[place], dp=peer)

    line_peers = [(z + near(k)) % NZ for k in range(1, NZ)]
    line_from = [(z + NZ - near(k)) % NZ for k in range(1, NZ)]
    plane_peers = [(q + k) % NQ for k in range(1, NQ)]
    dp_peers = [(mine + k) % dp for k in (1, 3, 2)]
    y_peers = [(y + k) % NY for k in (1, 3, 2)]

    load = pltpu.make_async_copy(table_ref, table.at[0:rows], table_sem)
    load.start()
    barrier = pltpu.get_barrier_semaphore()
    for peer in line_peers:
        pl.semaphore_signal(barrier, inc=1, device_id={"table": on_line(peer)}, device_id_type=MESH)
    for peer in plane_peers:
        pl.semaphore_signal(barrier, inc=1, device_id={"table": on_plane(peer)}, device_id_type=MESH)
    for peer in dp_peers:
        pl.semaphore_signal(barrier, inc=1, device_id={"dp": peer}, device_id_type=MESH)
    table[rows : rows + 8, :] = jnp.zeros((8, width), F32)
    total[...] = jnp.zeros_like(total)
    placed[...] = jnp.zeros_like(placed)

    def widen(i, carry):
        block = jnp.broadcast_to(accum_ref[pl.ds(i, 1), :], (128, 128))
        wide_accum[pl.ds(pl.multiple_of(i * 128, 128), 128), :] = block.T
        return carry

    lax.fori_loop(0, rows // 128, widen, 0)
    pl.semaphore_wait(barrier, len(line_peers) + len(plane_peers) + len(dp_peers))

    for peer in line_peers:
        code_copy(peer, z).start()
    for peer in line_peers:
        line_copy(peer, z).start()
    code_in[z] = code_ref[z]
    line_in[z] = grads_ref[...]

    slot = lax.broadcasted_iota(I32, (CAP, bags), 0)

    def pack(i, carry):
        s = (z + NZ - near(i)) % NZ

        @pl.when(i > 0)
        def _():
            code_copy(s, s).wait_recv()
            line_copy(s, s).wait_recv()

        grads = line_in[s]
        for k in range(1, NQ + 1):
            o = (q + k) % NQ
            code = code_in[s, pl.ds(o, 1), :]
            hot = slot == jnp.where(code < 0, -1, code & (CAP - 1))
            mark = hot.astype(F32).astype(BF16)
            marks[s, r_rows(o), :] = mark
            lines = jnp.dot(mark, grads, preferred_element_type=F32).astype(BF16)
            named = jnp.where(hot, (code >> 7) + 1, 0)
            named = sum(named[:, b : b + CAP] for b in range(0, bags, CAP))
            named = jnp.sum(named.T, axis=0, keepdims=True)
            named = jnp.where(named == 0, rows, named - 1)
            if k < NQ:
                q_out[pl.ds(o * NZ + s, 1), :] = named
                g_out[o, s] = lines
                g_copy(o, q, s).start()
            else:
                q_in[pl.ds(o * NZ + s, 1), :] = named
                g_in[o, s] = lines
        return carry

    lax.fori_loop(0, NZ, pack, 0)
    for peer in plane_peers:
        q_copy(peer, q).start()
    for peer in plane_peers:
        q_copy(peer, peer).wait_recv()
    fetch = pltpu.make_async_copy(q_in, q_smem, smem_sem)
    fetch.start()
    fetch.wait()
    load.wait()

    def pick(o, s):
        for i in range(CAP):
            line[pl.ds(i, 1), :] = table[pl.ds(q_smem[o * NZ + s, i], 1), :]
        return line[...].astype(BF16)

    def serve(i, carry):
        s = (z + near(NZ - 1 - i // NQ)) % NZ
        k = i % NQ
        o = (q + k) % NQ
        picked = pick(o, s)

        @pl.when(k == 0)
        def _():
            r_in[s, r_rows(o), :] = picked

        @pl.when(k > 0)
        def _():
            r_out[o, s] = picked
            r_copy(o, q, s).start()

        return carry

    lax.fori_loop(0, NZ * NQ, serve, 0)

    chunk = 256
    low_row = lax.broadcasted_iota(I32, (chunk, CAP), 0)

    def add(k, carry):
        o = (q + NQ - k) % NQ

        @pl.when(k > 0)
        def _():
            for s in range(NZ):
                g_copy(o, o, s).wait_recv()

        names = q_in[q_rows(o), :]
        low = names & (quarter - 1)
        high = (names // quarter).T
        grads = []
        for s in range(NZ):
            block = jnp.broadcast_to(high[:, s : s + 1], (CAP, width))
            mine_only = [(block == d).astype(F32).astype(BF16) * g_in[o, s] for d in range(dp)]
            grads.append(jnp.concatenate(mine_only, axis=1))
        grads = jnp.concatenate(grads, axis=0)
        for b in range(0, quarter, chunk):
            hot = jnp.concatenate(
                [(low_row == low[s : s + 1, :] - b).astype(F32).astype(BF16) for s in range(NZ)],
                axis=1,
            )
            total[b : b + chunk, :] += jnp.dot(hot, grads, preferred_element_type=F32)
        return carry

    lax.fori_loop(0, NQ, add, 0)
    for h in range(HALVES):
        for d in range(dp):
            part[d, half_rows(h), :] = total[half_rows(h), d * width : (d + 1) * width].astype(BF16)
        for peer in dp_peers:
            part_copy(peer, mine, h).start()

    def pool(i, carry):
        s = (z + near(NZ - 1 - i)) % NZ
        for k in range(1, NQ):
            o = (q + k) % NQ
            r_copy(o, o, s).wait_recv()
        pooled = lax.dot_general(
            r_in[s], marks[s], (((0,), (0,)), ((), ())), preferred_element_type=F32
        )
        pool_out[s] = pooled.astype(BF16)
        pool_copy(s, z).start()
        return carry

    for h in range(HALVES):
        summed = part[mine, half_rows(h), :].astype(F32)
        for peer in dp_peers:
            part_copy(peer, peer, h).wait_recv()
            summed = summed + quarter_in[peer, half_rows(h), :].astype(F32)
        sums[mine, half_rows(h), :] = summed.astype(BF16)
        for peer in dp_peers:
            sum_copy(peer, mine, h).start()

    lax.fori_loop(0, 4, pool, 0)

    slots = placed.shape[0]
    place_chunk = 256
    place_row = lax.broadcasted_iota(I32, (place_chunk, 128), 0)

    def update(d, h):
        base = pl.multiple_of(d * quarter + h * half, half)
        there = pl.ds(base, half)
        g = sums[d, half_rows(h), :].astype(F32)
        squares = jnp.sum(g * g, axis=1, keepdims=True) * (1.0 / width)
        accum = wide_accum[there, :] + squares
        wide_accum[there, :] = accum
        delta = g * (-LEARN) * lax.rsqrt(accum + EPSILON)
        new_table_ref[there, :] = table[there, :] + delta
        delta = delta.astype(BF16)
        lines = [slot_ref[pl.ds(base // 128 + i, 1), :] for i in range(half // 128)]
        for b in range(0, slots, place_chunk):
            hot = jnp.concatenate(
                [(place_row == one - b).astype(F32).astype(BF16) for one in lines], axis=1
            )
            placed[b : b + place_chunk, :] += jnp.dot(hot, delta, preferred_element_type=F32)

    for h in range(HALVES):
        update(mine, h)
    for h in range(HALVES):
        for peer in dp_peers:
            sum_copy(peer, peer, h).wait_recv()
            update(peer, h)

    per_core = slots // NC
    core_out[...] = placed[pl.ds(pl.multiple_of((1 - c) * per_core, per_core), per_core), :].astype(BF16)
    core_copy().start()
    kept = pl.ds(pl.multiple_of(c * per_core, per_core), per_core)
    core_copy().wait_recv()
    placed[kept, :] = placed[kept, :] + core_in[...].astype(F32)
    per_z = per_core // NZ
    for peer in line_peers:
        begin = pl.multiple_of(c * per_core + peer * per_z, per_z)
        z_out[peer] = placed[pl.ds(begin, per_z), :].astype(BF16)
        z_copy(peer, z).start()
    z_sum = placed[pl.ds(pl.multiple_of(c * per_core + z * per_z, per_z), per_z), :]
    lax.fori_loop(4, NZ - 1, pool, 0)
    for k in range(1, NQ):
        o = (q + k) % NQ
        r_copy(o, o, z).wait_recv()
    own_pool = lax.dot_general(
        r_in[z], marks[z], (((0,), (0,)), ((), ())), preferred_element_type=F32
    )
    for peer in line_from:
        z_copy(peer, peer).wait_recv()
        z_sum = z_sum + z_in[peer].astype(F32)
    per_y = per_z // NY
    for j in range(NY):
        y_in[NY + j] = z_sum[j * per_y : (j + 1) * per_y, :]
    for peer in y_peers:
        y_out[peer] = y_in[NY + peer]
        y_copy(peer, y).start()
    y_sum = y_in[NY + y]
    for peer in y_peers:
        y_copy(peer, peer).wait_recv()
        y_sum = y_sum + y_in[peer]
    x_part[mine] = y_sum
    for peer in dp_peers:
        x_copy(peer, mine).start()

    for peer in line_from:
        pool_copy(peer, peer).wait_recv()
        own_pool = own_pool + pool_in[peer].astype(F32)
    pooled_ref[...] = own_pool.T.astype(BF16)

    def narrow(i, carry):
        block = wide_accum[pl.ds(pl.multiple_of(i * 128, 128), 128), :]
        new_accum_ref[pl.ds(i, 1), :] = block.T[0:1, :]
        return carry

    lax.fori_loop(0, rows // 128, narrow, 0)
    for peer in dp_peers:
        x_copy(peer, peer).wait_recv()
    for d in range(dp):
        lines = slice(d * per_y, (d + 1) * per_y)
        new_parity_ref[lines, :] = parity_ref[lines, :] + x_part[d]

    core_copy().wait_send()
    for peer in line_peers:
        code_copy(peer, z).wait_send()
        line_copy(peer, z).wait_send()
        pool_copy(peer, z).wait_send()
        z_copy(peer, z).wait_send()

    def sent(k, carry):
        peer = (q + k) % NQ
        for s in range(NZ):
            g_copy(peer, q, s).wait_send()
            r_copy(peer, q, s).wait_send()
        q_copy(peer, q).wait_send()
        return carry

    lax.fori_loop(1, NQ, sent, 0)
    for peer in dp_peers:
        for h in range(HALVES):
            part_copy(peer, mine, h).wait_send()
            sum_copy(peer, mine, h).wait_send()
        x_copy(peer, mine).wait_send()
    for peer in y_peers:
        y_copy(peer, y).wait_send()


def on_device(owners, local_rows, grad_pooled, table, accum, parity, parity_slot):
    table_count, dp = lax.axis_size("table"), lax.axis_size("dp")
    bags = owners.shape[0]
    rows, width = table.shape
    mine = lax.axis_index("dp")

    index = jnp.arange(table_count, dtype=I32)
    owner_at = (index % NQ // NC * NZ + index // NQ) * NC + index % NC
    named = owners.T[:, None, :] == owner_at[None, :, None]
    hits = jnp.any(named, axis=0)
    wanted = jnp.sum(jnp.where(named, local_rows.T[:, None, :], 0), axis=0)
    before = jnp.arange(bags)[:, None] < jnp.arange(bags)[None, :]
    rank = jnp.dot(hits.astype(BF16), before.astype(BF16), preferred_element_type=F32)
    code = jnp.where(hits, wanted * CAP + rank.astype(I32), -1).reshape(NZ, NQ, bags)

    count = parity.shape[0]
    share = count // dp
    holder, place = parity_slot // count, parity_slot % count
    holder_y, holder_z, holder_c = holder // (NZ * NC), holder // NC % NZ, holder % NC
    order = (holder_c * NZ + holder_z) * NY + holder_y
    slot = jnp.where(place // share == mine, order * share + place % share, -1)
    slots = table_count * share

    quarter = rows // dp
    dma = pltpu.SemaphoreType.DMA
    pooled, new_table, new_accum, new_parity = pl.pallas_call(
        step_kernel,
        out_shape=(
            jax.ShapeDtypeStruct((bags, width), BF16),
            jax.ShapeDtypeStruct((rows, width), F32),
            jax.ShapeDtypeStruct((rows // 128, 128), F32),
            jax.ShapeDtypeStruct((count, width), F32),
        ),
        in_specs=[VMEM, VMEM, pl.BlockSpec(memory_space=pl.ANY), VMEM, VMEM, VMEM],
        out_specs=(VMEM,) * 4,
        scratch_shapes=[
            pltpu.VMEM((rows + 8, width), F32),
            pltpu.VMEM((rows, 128), F32),
            pltpu.VMEM((NZ, bags, width), BF16),
            pltpu.VMEM((NZ, NQ, bags), I32),
            pltpu.VMEM((NZ, NQ * CAP, bags), BF16),
            pltpu.VMEM((NQ, NZ, CAP, width), BF16),
            pltpu.VMEM((NQ, NZ, CAP, width), BF16),
            pltpu.VMEM((NQ * NZ, CAP), I32),
            pltpu.VMEM((NQ * NZ, CAP), I32),
            pltpu.SMEM((NQ * NZ, CAP), I32),
            pltpu.VMEM((NQ, NZ, CAP, width), BF16),
            pltpu.VMEM((NZ, NQ * CAP, width), BF16),
            pltpu.VMEM((quarter, dp * width), F32),
            pltpu.VMEM((dp, quarter, width), BF16),
            pltpu.VMEM((dp, quarter, width), BF16),
            pltpu.VMEM((dp, quarter, width), BF16),
            pltpu.VMEM((NZ, width, bags), BF16),
            pltpu.VMEM((NZ, width, bags), BF16),
            pltpu.VMEM((CAP, width), F32),
            pltpu.VMEM((slots, width), F32),
            pltpu.VMEM((slots // NC, width), BF16),
            pltpu.VMEM((slots // NC, width), BF16),
            pltpu.VMEM((NZ, NY * share, width), BF16),
            pltpu.VMEM((NZ, NY * share, width), BF16),
            pltpu.VMEM((NY, share, width), F32),
            pltpu.VMEM((2 * NY, share, width), F32),
            pltpu.VMEM((dp, share, width), F32),
        ]
        + [dma((NZ,))] * 4
        + [dma((NQ, NZ))] * 2
        + [dma((NQ,))] * 2
        + [dma((NQ, NZ))] * 2
        + [dma((dp, HALVES))] * 4
        + [dma((NZ,))] * 2
        + [dma] * 2
        + [dma((NZ,))] * 2
        + [dma((NY,))] * 2
        + [dma((dp,))] * 2
        + [dma, dma],
        compiler_params=pltpu.CompilerParams(
            vmem_limit_bytes=56 * 1024 * 1024, collective_id=0, has_side_effects=True
        ),
        name="step",
    )(
        code,
        grad_pooled,
        table,
        accum.reshape(rows // 128, 128),
        slot.reshape(rows // 128, 128),
        parity,
    )
    return (pooled, new_table, new_accum.reshape(rows), new_parity)


def solution(mesh):
    in_specs = (
        P(("table", "dp"), None),
        P(("table", "dp"), None),
        P(("table", "dp"), None),
        P("table", None),
        P("table"),
        P("table", None),
        P("table"),
    )
    out_specs = (P(("table", "dp"), None), P("table", None), P("table"), P("table", None))
    return jax.shard_map(
        on_device, mesh=mesh, in_specs=in_specs, out_specs=out_specs, check_vma=False
    )
```

```python
import jax
import jax.numpy as jnp
from jax import lax
from jax.experimental import pallas as pl
from jax.experimental.pallas import tpu as pltpu
from jax.sharding import PartitionSpec as P

LEARN = 0.5
EPSILON = 1e-06
F32, BF16, I32 = jnp.float32, jnp.bfloat16, jnp.int32
VMEM = pl.BlockSpec(memory_space=pltpu.VMEM)
MESH = pl.DeviceIdType.MESH
NY, NZ, NC = 4, 8, 2
NQ = NY * NC
CAP = 128
HALVES = 2
PIECES = 2


def near(k):
    j = (k + 1) // 2
    return (k % 2) * j + (1 - k % 2) * ((NZ - j) % NZ)


def step_kernel(
    code_ref, grads_ref, table_ref, accum_ref, slot_ref, parity_ref,
    pooled_ref, new_table_ref, new_accum_ref, new_parity_ref,
    table, wide_accum, line_in, code_in, marks, g_out, g_in, q_out, q_in, q_smem, r_out, r_in,
    total, part, quarter_in, sums, pool_out, pool_in, line, placed, core_out, core_in,
    z_out, z_in, y_out, y_in, x_part,
    code_s, code_r, line_s, line_r, g_s, g_r, q_s, q_r, r_s, r_r, part_s, part_r, sum_s, sum_r,
    pool_s, pool_r, core_s, core_r, z_s, z_r, y_s, y_r, x_s, x_r, table_sem, smem_sem,
):
    bags = code_ref.shape[2]
    rows, width = table_ref.shape
    dp = sums.shape[0]
    quarter = rows // dp
    half = quarter // HALVES
    me, mine = lax.axis_index("table"), lax.axis_index("dp")
    z, c, y = (me // NC) % NZ, me % NC, me // (NC * NZ)
    q = y * NC + c

    def remote(src, dst, send, recv, **where):
        return pltpu.make_async_remote_copy(
            src_ref=src, dst_ref=dst, send_sem=send, recv_sem=recv, device_id=where,
            device_id_type=MESH,
        )

    def on_line(other):
        return (me - z * NC) + other * NC

    def on_plane(other):
        return (other // NC) * (NZ * NC) + z * NC + other % NC

    def code_copy(peer, place):
        return remote(code_ref.at[peer], code_in.at[place], code_s.at[peer], code_r.at[place],
                      table=on_line(peer))

    piece = bags // PIECES

    def line_copy(way, hop, origin, i):
        block = line_in.at[origin, pl.ds(i * piece, piece)]
        return remote(block, block, line_s.at[way, hop, i], line_r.at[origin, i],
                      table=on_line((z + 1 + way * (NZ - 2)) % NZ))

    def r_rows(o):
        return pl.ds(pl.multiple_of(o * CAP, CAP), CAP)

    def g_copy(peer, place, s):
        return remote(g_out.at[s, r_rows(peer)], g_in.at[s, r_rows(place)], g_s.at[peer, s],
                      g_r.at[place, s], table=on_plane(peer))

    def q_copy(peer, place, s):
        return remote(q_out.at[s, peer], q_in.at[s, place], q_s.at[peer, s], q_r.at[place, s],
                      table=on_plane(peer))

    def r_copy(peer, place, s):
        return remote(r_out.at[peer, s], r_in.at[s, r_rows(place)], r_s.at[peer, s],
                      r_r.at[place, s], table=on_plane(peer))

    def half_rows(h):
        return pl.ds(h * half, half)

    def part_copy(peer, place, h):
        return remote(part.at[peer, half_rows(h)], quarter_in.at[place, half_rows(h)],
                      part_s.at[peer, h], part_r.at[place, h], dp=peer)

    def sum_copy(peer, place, h):
        return remote(sums.at[place, half_rows(h)], sums.at[place, half_rows(h)],
                      sum_s.at[peer, h], sum_r.at[place, h], dp=peer)

    def pool_copy(peer, place):
        return remote(pool_out.at[peer], pool_in.at[place], pool_s.at[peer], pool_r.at[place],
                      table=on_line(peer))

    def core_copy():
        return remote(core_out, core_in, core_s, core_r, table=me + 1 - 2 * c)

    def z_copy(peer, place):
        return remote(z_out.at[peer], z_in.at[place], z_s.at[peer], z_r.at[place],
                      table=on_line(peer))

    def y_copy(peer, place):
        return remote(y_out.at[peer], y_in.at[place], y_s.at[peer], y_r.at[place],
                      table=on_plane(peer * NC + c))

    def x_copy(peer, place):
        return remote(x_part.at[place], x_part.at[place], x_s.at[peer], x_r.at[place], dp=peer)

    line_peers = [(z + near(k)) % NZ for k in range(1, NZ)]
    line_from = [(z + NZ - near(k)) % NZ for k in range(1, NZ)]
    plane_peers = [(q + k) % NQ for k in range(1, NQ)]
    dp_peers = [(mine + k) % dp for k in (1, 3, 2)]
    y_peers = [(y + k) % NY for k in (1, 3, 2)]

    load = pltpu.make_async_copy(table_ref, table.at[0:rows], table_sem)
    load.start()
    barrier = pltpu.get_barrier_semaphore()
    for peer in line_peers:
        pl.semaphore_signal(barrier, inc=1, device_id={"table": on_line(peer)}, device_id_type=MESH)
    for peer in plane_peers:
        pl.semaphore_signal(barrier, inc=1, device_id={"table": on_plane(peer)}, device_id_type=MESH)
    for peer in dp_peers:
        pl.semaphore_signal(barrier, inc=1, device_id={"dp": peer}, device_id_type=MESH)
    table[rows : rows + 8, :] = jnp.zeros((8, width), F32)
    total[...] = jnp.zeros_like(total)
    placed[...] = jnp.zeros_like(placed)

    def widen(i, carry):
        block = jnp.broadcast_to(accum_ref[pl.ds(i, 1), :], (128, 128))
        wide_accum[pl.ds(pl.multiple_of(i * 128, 128), 128), :] = block.T
        return carry

    lax.fori_loop(0, rows // 128, widen, 0)
    pl.semaphore_wait(barrier, len(line_peers) + len(plane_peers) + len(dp_peers))

    for peer in line_peers:
        code_copy(peer, z).start()
    line_in[z] = grads_ref[...]
    for i in range(PIECES):
        for way in (0, 1):
            line_copy(way, 0, z, i).start()
    code_in[z] = code_ref[z]

    slot = lax.broadcasted_iota(I32, (CAP, bags), 0)

    def pack(i):
        s = (z + NZ - near(i)) % NZ

        @pl.when(i > 0)
        def _():
            code_copy(s, s).wait_recv()

        for o in range(NQ):
            code = code_in[s, o : o + 1, :]
            hot = slot == jnp.where(code < 0, -1, code & (CAP - 1))
            marks[s, o * CAP : (o + 1) * CAP, :] = hot.astype(F32).astype(BF16)
            named = jnp.where(hot, (code >> 7) + 1, 0)
            named = sum(named[:, b : b + CAP] for b in range(0, bags, CAP))
            named = jnp.sum(named.T, axis=0, keepdims=True)
            q_out[s, o] = jnp.where(named == 0, rows, named - 1)
        for peer in plane_peers:
            q_copy(peer, q, s).start()
        q_in[s, q] = q_out[s, q]
        g_out[s] = jnp.dot(marks[s], line_in[s], preferred_element_type=F32).astype(BF16)
        for peer in plane_peers:
            g_copy(peer, q, s).start()
        g_in[s, r_rows(q), :] = g_out[s, r_rows(q), :]

    def pass_on(h):
        for i in range(PIECES):
            for way, last in ((0, NZ // 2), (1, NZ // 2 - 1)):
                origin = (z + NZ - h + way * 2 * h) % NZ

                @pl.when(h <= last)
                def _():
                    line_copy(way, 0, origin, i).wait_recv()

                @pl.when(h < last)
                def _():
                    line_copy(way, h, origin, i).start()

    chunk = 256
    low_row = lax.broadcasted_iota(I32, (chunk, CAP), 0)

    def add(i):
        s = (z + NZ - near(i)) % NZ
        for k in range(1, NQ):
            o = (q + k) % NQ
            q_copy(o, o, s).wait_recv()
            g_copy(o, o, s).wait_recv()
        names = [q_in[s, o] for o in range(NQ)]
        high = (jnp.concatenate(names, axis=0) // quarter).T
        grads = []
        for o in range(NQ):
            block = jnp.broadcast_to(high[:, o : o + 1], (CAP, width))
            lines = g_in[s, o * CAP : (o + 1) * CAP, :]
            grads.append(
                jnp.concatenate([(block == d).astype(F32).astype(BF16) * lines for d in range(dp)], axis=1)
            )
        grads = jnp.concatenate(grads, axis=0)
        low = [one & (quarter - 1) for one in names]
        for b in range(0, quarter, chunk):
            hot = jnp.concatenate(
                [(low_row == one - b).astype(F32).astype(BF16) for one in low], axis=1
            )
            total[b : b + chunk, :] += jnp.dot(hot, grads, preferred_element_type=F32)

    def relay(p, carry):
        def packs(i, carry):
            pl.when(jnp.logical_and(i >= 0, i < NZ))(lambda: pack(i))
            return carry

        def adds(i, carry):
            pl.when(i >= 0)(lambda: add(i))
            return carry

        lax.fori_loop(2 * p - 1, 2 * p + 1, packs, 0)
        pass_on(p + 1)
        lax.fori_loop(2 * p - 3, 2 * p - 1, adds, 0)
        return carry

    lax.fori_loop(0, NZ // 2 + 1, relay, 0)
    add(NZ - 1)
    for h in range(HALVES):
        for d in range(dp):
            part[d, half_rows(h), :] = total[half_rows(h), d * width : (d + 1) * width].astype(BF16)
        for peer in dp_peers:
            part_copy(peer, mine, h).start()

    fetch = pltpu.make_async_copy(q_in, q_smem, smem_sem)
    fetch.start()
    fetch.wait()
    load.wait()

    def pick(o, s):
        for i in range(CAP):
            line[pl.ds(i, 1), :] = table[pl.ds(q_smem[s, o, 0, i], 1), :]
        return line[...].astype(BF16)

    def serve(i, carry):
        s = (z + near(NZ - 1 - i // NQ)) % NZ
        k = i % NQ
        o = (q + k) % NQ
        picked = pick(o, s)

        @pl.when(k == 0)
        def _():
            r_in[s, r_rows(o), :] = picked

        @pl.when(k > 0)
        def _():
            r_out[o, s] = picked
            r_copy(o, q, s).start()

        return carry

    lax.fori_loop(0, NZ * NQ, serve, 0)

    def pool(i, carry):
        s = (z + near(NZ - 1 - i)) % NZ
        for k in range(1, NQ):
            o = (q + k) % NQ
            r_copy(o, o, s).wait_recv()
        pooled = lax.dot_general(
            r_in[s], marks[s], (((0,), (0,)), ((), ())), preferred_element_type=F32
        )
        pool_out[s] = pooled.astype(BF16)
        pool_copy(s, z).start()
        return carry

    for h in range(HALVES):
        summed = part[mine, half_rows(h), :].astype(F32)
        for peer in dp_peers:
            part_copy(peer, peer, h).wait_recv()
            summed = summed + quarter_in[peer, half_rows(h), :].astype(F32)
        sums[mine, half_rows(h), :] = summed.astype(BF16)
        for peer in dp_peers:
            sum_copy(peer, mine, h).start()

    slots = placed.shape[0]
    place_chunk = 256
    place_row = lax.broadcasted_iota(I32, (place_chunk, 128), 0)

    def update(d, h):
        base = pl.multiple_of(d * quarter + h * half, half)
        there = pl.ds(base, half)
        g = sums[d, half_rows(h), :].astype(F32)
        squares = jnp.sum(g * g, axis=1, keepdims=True) * (1.0 / width)
        accum = wide_accum[there, :] + squares
        wide_accum[there, :] = accum
        delta = g * (-LEARN) * lax.rsqrt(accum + EPSILON)
        new_table_ref[there, :] = table[there, :] + delta
        delta = delta.astype(BF16)
        lines = [slot_ref[pl.ds(base // 128 + i, 1), :] for i in range(half // 128)]
        for b in range(0, slots, place_chunk):
            hot = jnp.concatenate(
                [(place_row == one - b).astype(F32).astype(BF16) for one in lines], axis=1
            )
            placed[b : b + place_chunk, :] += jnp.dot(hot, delta, preferred_element_type=F32)

    for h in range(HALVES):
        update(mine, h)
    lax.fori_loop(0, 4, pool, 0)
    for h in range(HALVES):
        for peer in dp_peers:
            sum_copy(peer, peer, h).wait_recv()
            update(peer, h)

    per_core = slots // NC
    core_out[...] = placed[pl.ds(pl.multiple_of((1 - c) * per_core, per_core), per_core), :].astype(BF16)
    core_copy().start()
    kept = pl.ds(pl.multiple_of(c * per_core, per_core), per_core)
    core_copy().wait_recv()
    placed[kept, :] = placed[kept, :] + core_in[...].astype(F32)
    per_z = per_core // NZ
    for peer in line_peers:
        begin = pl.multiple_of(c * per_core + peer * per_z, per_z)
        z_out[peer] = placed[pl.ds(begin, per_z), :].astype(BF16)
        z_copy(peer, z).start()
    z_sum = placed[pl.ds(pl.multiple_of(c * per_core + z * per_z, per_z), per_z), :]
    lax.fori_loop(4, NZ - 1, pool, 0)
    for k in range(1, NQ):
        o = (q + k) % NQ
        r_copy(o, o, z).wait_recv()
    own_pool = lax.dot_general(
        r_in[z], marks[z], (((0,), (0,)), ((), ())), preferred_element_type=F32
    )
    for peer in line_from:
        z_copy(peer, peer).wait_recv()
        z_sum = z_sum + z_in[peer].astype(F32)
    per_y = per_z // NY
    for j in range(NY):
        y_in[NY + j] = z_sum[j * per_y : (j + 1) * per_y, :]
    for peer in y_peers:
        y_out[peer] = y_in[NY + peer]
        y_copy(peer, y).start()
    y_sum = y_in[NY + y]
    for peer in y_peers:
        y_copy(peer, peer).wait_recv()
        y_sum = y_sum + y_in[peer]
    x_part[mine] = y_sum
    for peer in dp_peers:
        x_copy(peer, mine).start()

    for peer in line_from:
        pool_copy(peer, peer).wait_recv()
        own_pool = own_pool + pool_in[peer].astype(F32)
    pooled_ref[...] = own_pool.T.astype(BF16)

    def narrow(i, carry):
        block = wide_accum[pl.ds(pl.multiple_of(i * 128, 128), 128), :]
        new_accum_ref[pl.ds(i, 1), :] = block.T[0:1, :]
        return carry

    lax.fori_loop(0, rows // 128, narrow, 0)
    for peer in dp_peers:
        x_copy(peer, peer).wait_recv()
    for d in range(dp):
        lines = slice(d * per_y, (d + 1) * per_y)
        new_parity_ref[lines, :] = parity_ref[lines, :] + x_part[d]

    core_copy().wait_send()
    for peer in line_peers:
        code_copy(peer, z).wait_send()
        pool_copy(peer, z).wait_send()
        z_copy(peer, z).wait_send()

    for i in range(PIECES):
        for hop in range(NZ // 2):
            line_copy(0, hop, z, i).wait_send()
        for hop in range(NZ // 2 - 1):
            line_copy(1, hop, z, i).wait_send()

    def sent(k, carry):
        peer = (q + k) % NQ
        for s in range(NZ):
            g_copy(peer, q, s).wait_send()
            r_copy(peer, q, s).wait_send()
            q_copy(peer, q, s).wait_send()
        return carry

    lax.fori_loop(1, NQ, sent, 0)
    for peer in dp_peers:
        for h in range(HALVES):
            part_copy(peer, mine, h).wait_send()
            sum_copy(peer, mine, h).wait_send()
        x_copy(peer, mine).wait_send()
    for peer in y_peers:
        y_copy(peer, y).wait_send()


def on_device(owners, local_rows, grad_pooled, table, accum, parity, parity_slot):
    table_count, dp = lax.axis_size("table"), lax.axis_size("dp")
    bags = owners.shape[0]
    rows, width = table.shape
    mine = lax.axis_index("dp")

    index = jnp.arange(table_count, dtype=I32)
    owner_at = (index % NQ // NC * NZ + index // NQ) * NC + index % NC
    named = owners.T[:, None, :] == owner_at[None, :, None]
    hits = jnp.any(named, axis=0)
    wanted = jnp.sum(jnp.where(named, local_rows.T[:, None, :], 0), axis=0)
    before = jnp.arange(bags)[:, None] < jnp.arange(bags)[None, :]
    rank = jnp.dot(hits.astype(BF16), before.astype(BF16), preferred_element_type=F32)
    code = jnp.where(hits, wanted * CAP + rank.astype(I32), -1).reshape(NZ, NQ, bags)

    count = parity.shape[0]
    share = count // dp
    holder, place = parity_slot // count, parity_slot % count
    holder_y, holder_z, holder_c = holder // (NZ * NC), holder // NC % NZ, holder % NC
    order = (holder_c * NZ + holder_z) * NY + holder_y
    slot = jnp.where(place // share == mine, order * share + place % share, -1)
    slots = table_count * share

    quarter = rows // dp
    dma = pltpu.SemaphoreType.DMA
    pooled, new_table, new_accum, new_parity = pl.pallas_call(
        step_kernel,
        out_shape=(
            jax.ShapeDtypeStruct((bags, width), BF16),
            jax.ShapeDtypeStruct((rows, width), F32),
            jax.ShapeDtypeStruct((rows // 128, 128), F32),
            jax.ShapeDtypeStruct((count, width), F32),
        ),
        in_specs=[VMEM, VMEM, pl.BlockSpec(memory_space=pl.ANY), VMEM, VMEM, VMEM],
        out_specs=(VMEM,) * 4,
        scratch_shapes=[
            pltpu.VMEM((rows + 8, width), F32),
            pltpu.VMEM((rows, 128), F32),
            pltpu.VMEM((NZ, bags, width), BF16),
            pltpu.VMEM((NZ, NQ, bags), I32),
            pltpu.VMEM((NZ, NQ * CAP, bags), BF16),
            pltpu.VMEM((NZ, NQ * CAP, width), BF16),
            pltpu.VMEM((NZ, NQ * CAP, width), BF16),
            pltpu.VMEM((NZ, NQ, 1, CAP), I32),
            pltpu.VMEM((NZ, NQ, 1, CAP), I32),
            pltpu.SMEM((NZ, NQ, 1, CAP), I32),
            pltpu.VMEM((NQ, NZ, CAP, width), BF16),
            pltpu.VMEM((NZ, NQ * CAP, width), BF16),
            pltpu.VMEM((quarter, dp * width), F32),
            pltpu.VMEM((dp, quarter, width), BF16),
            pltpu.VMEM((dp, quarter, width), BF16),
            pltpu.VMEM((dp, quarter, width), BF16),
            pltpu.VMEM((NZ, width, bags), BF16),
            pltpu.VMEM((NZ, width, bags), BF16),
            pltpu.VMEM((CAP, width), F32),
            pltpu.VMEM((slots, width), F32),
            pltpu.VMEM((slots // NC, width), BF16),
            pltpu.VMEM((slots // NC, width), BF16),
            pltpu.VMEM((NZ, NY * share, width), BF16),
            pltpu.VMEM((NZ, NY * share, width), BF16),
            pltpu.VMEM((NY, share, width), F32),
            pltpu.VMEM((2 * NY, share, width), F32),
            pltpu.VMEM((dp, share, width), F32),
        ]
        + [dma((NZ,))] * 2
        + [dma((2, NZ // 2, PIECES)), dma((NZ, PIECES))]
        + [dma((NQ, NZ))] * 6
        + [dma((dp, HALVES))] * 4
        + [dma((NZ,))] * 2
        + [dma] * 2
        + [dma((NZ,))] * 2
        + [dma((NY,))] * 2
        + [dma((dp,))] * 2
        + [dma, dma],
        compiler_params=pltpu.CompilerParams(
            vmem_limit_bytes=56 * 1024 * 1024, collective_id=0, has_side_effects=True
        ),
        name="step",
    )(
        code,
        grad_pooled,
        table,
        accum.reshape(rows // 128, 128),
        slot.reshape(rows // 128, 128),
        parity,
    )
    return (pooled, new_table, new_accum.reshape(rows), new_parity)


def solution(mesh):
    in_specs = (
        P(("table", "dp"), None),
        P(("table", "dp"), None),
        P(("table", "dp"), None),
        P("table", None),
        P("table"),
        P("table", None),
        P("table"),
    )
    out_specs = (P(("table", "dp"), None), P("table", None), P("table"), P("table", None))
    return jax.shard_map(
        on_device, mesh=mesh, in_specs=in_specs, out_specs=out_specs, check_vma=False
    )
```

```python
import jax
import jax.numpy as jnp
from jax import lax
from jax.experimental import pallas as pl
from jax.experimental.pallas import tpu as pltpu
from jax.sharding import PartitionSpec as P

LEARN = 0.5
EPSILON = 1e-06
F32, BF16, I32 = jnp.float32, jnp.bfloat16, jnp.int32
ANY = pl.BlockSpec(memory_space=pl.ANY)
VMEM = pl.BlockSpec(memory_space=pltpu.VMEM)
MESH = pl.DeviceIdType.MESH
NY, NZ, NC = 4, 8, 2
NQ = NY * NC
CAP = 128
HALVES = 2
PIECES = 2


def near(k):
    j = (k + 1) // 2
    return (k % 2) * j + (1 - k % 2) * ((NZ - j) % NZ)


def step_kernel(
    code_ref, grads_ref, table_ref, accum_ref, home_ref,
    pooled_ref, fresh_ref, new_accum_ref, change_ref,
    slot_ref, table, wide_accum, line_in, code_in, marks, g_out, g_in, q_out, q_in, q_smem, r_out, r_in,
    total, part, quarter_in, sums, pool_out, pool_in, line, placed, core_out, core_in,
    z_out, z_in, z_sums, y_out, y_in, x_part,
    code_s, code_r, line_s, line_r, g_s, g_r, q_s, q_r, r_s, r_r, part_s, part_r, sum_s, sum_r,
    pool_s, pool_r, core_s, core_r, z_s, z_r, y_s, y_r, x_s, x_r, table_sem, smem_sem, fresh, fresh_sem,
):
    bags = code_ref.shape[2]
    rows, width = table_ref.shape
    dp = sums.shape[0]
    quarter = rows // dp
    half = quarter // HALVES
    me, mine = lax.axis_index("table"), lax.axis_index("dp")
    z, c, y = (me // NC) % NZ, me % NC, me // (NC * NZ)
    q = y * NC + c

    def remote(src, dst, send, recv, **where):
        return pltpu.make_async_remote_copy(
            src_ref=src, dst_ref=dst, send_sem=send, recv_sem=recv, device_id=where,
            device_id_type=MESH,
        )

    def on_line(other):
        return (me - z * NC) + other * NC

    def on_plane(other):
        return (other // NC) * (NZ * NC) + z * NC + other % NC

    def code_copy(peer, place):
        return remote(code_ref.at[peer], code_in.at[place], code_s.at[peer], code_r.at[place],
                      table=on_line(peer))

    piece = bags // PIECES

    def line_copy(way, hop, origin, i):
        block = line_in.at[origin, pl.ds(i * piece, piece)]
        return remote(block, block, line_s.at[way, hop, i], line_r.at[origin, i],
                      table=on_line((z + 1 + way * (NZ - 2)) % NZ))

    def r_rows(o):
        return pl.ds(pl.multiple_of(o * CAP, CAP), CAP)

    def g_copy(peer, place, s):
        return remote(g_out.at[s, r_rows(peer)], g_in.at[s, r_rows(place)], g_s.at[s],
                      g_r.at[s], table=on_plane(peer))

    def q_copy(peer, place, s):
        return remote(q_out.at[s, peer], q_in.at[s, place], q_s.at[s], q_r.at[s],
                      table=on_plane(peer))

    def r_copy(peer, place, s):
        return remote(r_out.at[s, r_rows(peer)], r_in.at[s, r_rows(place)], r_s.at[s],
                      r_r.at[s], table=on_plane(peer))

    others = pl.ds(0, NQ - 1)
    other_rows = pl.ds(0, (NQ - 1) * CAP)

    def all_g(s):
        return remote(g_out.at[s, other_rows], g_in.at[s, other_rows], g_s.at[s], g_r.at[s],
                      table=on_plane((q + 1) % NQ))

    def all_q(s):
        return remote(q_out.at[s, others], q_in.at[s, others], q_s.at[s], q_r.at[s],
                      table=on_plane((q + 1) % NQ))

    def all_r(s):
        return remote(r_out.at[s, other_rows], r_in.at[s, other_rows], r_s.at[s], r_r.at[s],
                      table=on_plane((q + 1) % NQ))

    def half_rows(h):
        return pl.ds(h * half, half)

    def part_copy(peer, place, h):
        return remote(part.at[peer, half_rows(h)], quarter_in.at[place, half_rows(h)],
                      part_s.at[peer, h], part_r.at[place, h], dp=peer)

    def sum_copy(peer, place, h):
        return remote(sums.at[place, half_rows(h)], sums.at[place, half_rows(h)],
                      sum_s.at[peer, h], sum_r.at[place, h], dp=peer)

    def pool_copy(peer, place):
        return remote(pool_out.at[peer], pool_in.at[place], pool_s.at[peer], pool_r.at[place],
                      table=on_line(peer))

    def core_copy():
        return remote(core_out, core_in, core_s, core_r, table=me + 1 - 2 * c)

    def z_copy(peer, place):
        return remote(z_out.at[peer], z_in.at[place], z_s.at[peer], z_r.at[place],
                      table=on_line(peer))

    def y_copy(peer, place):
        return remote(y_out.at[peer], y_in.at[place], y_s.at[peer], y_r.at[place],
                      table=on_plane(peer * NC + c))

    def x_copy(peer, place):
        return remote(x_part.at[place], x_part.at[place], x_s.at[peer], x_r.at[place], dp=peer)

    line_peers = [(z + near(k)) % NZ for k in range(1, NZ)]
    line_from = [(z + NZ - near(k)) % NZ for k in range(1, NZ)]
    plane_peers = [(q + k) % NQ for k in range(1, NQ)]
    dp_peers = [(mine + k) % dp for k in (1, 3, 2)]
    right, left, far = [(mine + k) % dp for k in (1, dp - 1, 2)]
    y_peers = [(y + k) % NY for k in (1, 3, 2)]

    load = pltpu.make_async_copy(table_ref, table.at[0:rows], table_sem)
    load.start()
    barrier = pltpu.get_barrier_semaphore()
    for peer in line_peers:
        pl.semaphore_signal(barrier, inc=1, device_id={"table": on_line(peer)}, device_id_type=MESH)
    for peer in plane_peers:
        pl.semaphore_signal(barrier, inc=1, device_id={"table": on_plane(peer)}, device_id_type=MESH)
    for peer in dp_peers:
        pl.semaphore_signal(barrier, inc=1, device_id={"dp": peer}, device_id_type=MESH)

    pl.semaphore_wait(barrier, len(line_peers) + len(plane_peers) + len(dp_peers))
    line_in[z] = grads_ref[...]
    for i in range(PIECES):
        for way in (0, 1):
            line_copy(way, 0, z, i).start()
    for peer in line_peers:
        code_copy(peer, z).start()
    code_in[z] = code_ref[z]

    slot = lax.broadcasted_iota(I32, (CAP, bags), 0)

    def pack(i):
        s = (z + NZ - near(i)) % NZ

        @pl.when(i > 0)
        def _():
            code_copy(s, s).wait_recv()

        for o in range(NQ):
            code = code_in[s, o : o + 1, :]
            hot = slot == jnp.where(code < 0, -1, code & (CAP - 1))
            marks[s, o * CAP : (o + 1) * CAP, :] = hot.astype(F32).astype(BF16)
            named = jnp.where(hot, (code >> 7) + 1, 0)
            named = sum(named[:, b : b + CAP] for b in range(0, bags, CAP))
            named = jnp.sum(named.T, axis=0, keepdims=True)
            q_out[s, o] = jnp.where(named == 0, rows, named - 1)
        for peer in plane_peers:
            q_copy(peer, q, s).start()
        q_in[s, q] = q_out[s, q]
        g_out[s] = jnp.dot(marks[s], line_in[s], preferred_element_type=F32).astype(BF16)
        for peer in plane_peers:
            g_copy(peer, q, s).start()
        g_in[s, r_rows(q), :] = g_out[s, r_rows(q), :]

    def pass_on(h):
        for i in range(PIECES):
            for way, last in ((0, NZ // 2), (1, NZ // 2 - 1)):
                origin = (z + NZ - h + way * 2 * h) % NZ

                @pl.when(h <= last)
                def _():
                    line_copy(way, 0, origin, i).wait_recv()

                @pl.when(h < last)
                def _():
                    line_copy(way, h, origin, i).start()

    chunk = 256
    low_row = lax.broadcasted_iota(I32, (chunk, CAP), 0)

    def add(i):
        s = (z + NZ - near(i)) % NZ
        all_q(s).wait_recv()
        all_g(s).wait_recv()
        names = [q_in[s, o] for o in range(NQ)]
        high = (jnp.concatenate(names, axis=0) // quarter).T
        grads = []
        for o in range(NQ):
            block = jnp.broadcast_to(high[:, o : o + 1], (CAP, width))
            lines = g_in[s, o * CAP : (o + 1) * CAP, :]
            grads.append(
                jnp.concatenate([(block == d).astype(F32).astype(BF16) * lines for d in range(dp)], axis=1)
            )
        grads = jnp.concatenate(grads, axis=0)
        low = [one & (quarter - 1) for one in names]
        for b in range(0, quarter, chunk):
            hot = jnp.concatenate(
                [(low_row == one - b).astype(F32).astype(BF16) for one in low], axis=1
            )
            total[b : b + chunk, :] += jnp.dot(hot, grads, preferred_element_type=F32)

    share = change_ref.shape[0] // dp

    def prepare():
        count = change_ref.shape[0]
        home = home_ref[...]
        holder, place = home // count, home % count
        order = (holder % NC * NY + holder // (NZ * NC)) * NZ + holder // NC % NZ
        slot_ref[...] = jnp.where(place // share == mine, order * share + place % share, -1)

        table[rows : rows + 8, :] = jnp.zeros((8, width), F32)
        total[...] = jnp.zeros_like(total)
        placed[...] = jnp.zeros_like(placed)

        def widen(i, carry):
            block = jnp.broadcast_to(accum_ref[pl.ds(i, 1), :], (128, 128))
            wide_accum[pl.ds(pl.multiple_of(i * 128, 128), 128), :] = block.T
            return carry

        lax.fori_loop(0, rows // 128, widen, 0)

    def relay(p, carry):
        def packs(i, carry):
            pl.when(jnp.logical_and(i >= 0, i < NZ))(lambda: pack(i))
            return carry

        def adds(i, carry):
            add(i)
            return carry

        lax.fori_loop(2 * p - 1, 2 * p + 1, packs, 0)
        pl.when(p == 0)(prepare)
        pass_on(p + 1)
        lax.fori_loop(jnp.maximum(2 * p - 3, 0), jnp.maximum(2 * p - 1, 0), adds, 0)
        return carry

    lax.fori_loop(0, NZ // 2 + 1, relay, 0)
    lax.fori_loop(NZ - 1, NZ, lambda i, carry: (add(i), carry)[1], 0)
    def part_start(h):
        for d in range(dp):
            part[d, half_rows(h), :] = total[half_rows(h), d * width : (d + 1) * width].astype(BF16)
        for peer in dp_peers:
            part_copy(peer, mine, h).start()

    part_start(0)

    fetch = pltpu.make_async_copy(q_in, q_smem, smem_sem)
    fetch.start()
    fetch.wait()
    load.wait()

    def pick(o, s):
        for i in range(CAP):
            line[pl.ds(i, 1), :] = table[pl.ds(q_smem[s, o, 0, i], 1), :]
        return line[...].astype(BF16)

    def serve(j):
        s = (z + near(NZ - 1 - j)) % NZ

        def one(k, carry):
            o = (q + k) % NQ
            r_out[s, r_rows(o), :] = pick(o, s)
            r_copy(o, q, s).start()
            return carry

        lax.fori_loop(1, NQ, one, 0)
        r_in[s, r_rows(q), :] = pick(q, s)

    def pool(i, carry):
        s = (z + near(NZ - 1 - i)) % NZ
        all_r(s).wait_recv()
        pooled = lax.dot_general(
            r_in[s], marks[s], (((0,), (0,)), ((), ())), preferred_element_type=F32
        )
        pool_out[s] = pooled.astype(BF16)
        pool_copy(s, z).start()
        return carry


    def dp_sum(h):
        summed = part[mine, half_rows(h), :].astype(F32)
        for peer in dp_peers:
            part_copy(peer, peer, h).wait_recv()
            summed = summed + quarter_in[peer, half_rows(h), :].astype(F32)
        sums[mine, half_rows(h), :] = summed.astype(BF16)
        for peer in (right, left):
            sum_copy(peer, mine, h).start()

    def serves(j, carry):
        serve(j)

        @pl.when(j >= 4)
        def _():
            pool(j - 4, 0)

        return carry

    lax.fori_loop(0, 4, serves, 0)
    part_start(1)
    lax.fori_loop(4, 5, serves, 0)
    dp_sum(0)
    lax.fori_loop(5, NZ, serves, 0)
    dp_sum(1)

    slots = placed.shape[0]
    place_chunk = 256
    place_row = lax.broadcasted_iota(I32, (place_chunk, 128), 0)

    def fresh_copy(d, h):
        there = pl.ds(pl.multiple_of(d * quarter + h * half, half), half)
        return pltpu.make_async_copy(fresh.at[there], fresh_ref.at[there], fresh_sem.at[d, h])

    def update(d, h):
        base = pl.multiple_of(d * quarter + h * half, half)
        there = pl.ds(base, half)
        g = sums[d, half_rows(h), :].astype(F32)
        squares = jnp.sum(g * g, axis=1, keepdims=True) * (1.0 / width)
        accum = wide_accum[there, :] + squares
        wide_accum[there, :] = accum
        delta = g * (-LEARN) * lax.rsqrt(accum + EPSILON)
        fresh[there, :] = table[there, :] + delta
        fresh_copy(d, h).start()
        delta = delta.astype(BF16)
        lines = [slot_ref[pl.ds(base // 128 + i, 1), :] for i in range(half // 128)]
        for b in range(0, slots, place_chunk):
            hot = jnp.concatenate(
                [(place_row == one - b).astype(F32).astype(BF16) for one in lines], axis=1
            )
            placed[b : b + place_chunk, :] += jnp.dot(hot, delta, preferred_element_type=F32)

    def pass_sum(origin, peer, h):
        block = sums.at[origin, half_rows(h)]
        return remote(block, block, sum_s.at[far, h], sum_r.at[origin, h], dp=peer)

    def arrived(d, h):
        sum_copy(d, d, h).wait_recv()
        if d is left and h == 0:
            pass_sum(left, right, 0).start()
        if d is right and h == 1:
            pass_sum(right, left, 1).start()
        update(d, h)

    update(mine, 0)
    arrived(left, 0)
    arrived(right, 0)
    update(mine, 1)
    arrived(right, 1)
    arrived(left, 1)
    lax.fori_loop(4, 6, pool, 0)
    arrived(far, 0)
    arrived(far, 1)

    per_core = slots // NC
    core_out[...] = placed[pl.ds(pl.multiple_of((1 - c) * per_core, per_core), per_core), :].astype(BF16)
    core_copy().start()
    kept = pl.ds(pl.multiple_of(c * per_core, per_core), per_core)
    core_copy().wait_recv()
    placed[kept, :] = placed[kept, :] + core_in[...].astype(F32)
    per_y = per_core // NY
    for peer in y_peers:
        begin = pl.multiple_of(c * per_core + peer * per_y, per_y)
        y_out[peer] = placed[pl.ds(begin, per_y), :].astype(BF16)
        y_copy(peer, y).start()
    y_sum = placed[pl.ds(pl.multiple_of(c * per_core + y * per_y, per_y), per_y), :]
    lax.fori_loop(6, NZ - 1, pool, 0)
    for peer in y_peers:
        y_copy(peer, peer).wait_recv()
        y_sum = y_sum + y_in[peer].astype(F32)
    for k in range(NZ):
        z_sums[k] = y_sum[k * share : (k + 1) * share, :]
    for peer in line_peers:
        z_out[peer] = z_sums[peer].astype(BF16)
        z_copy(peer, z).start()
    all_r(z).wait_recv()
    own_pool = lax.dot_general(
        r_in[z], marks[z], (((0,), (0,)), ((), ())), preferred_element_type=F32
    )

    def narrow(i, carry):
        block = wide_accum[pl.ds(pl.multiple_of(i * 128, 128), 128), :]
        new_accum_ref[pl.ds(i, 1), :] = block.T[0:1, :]
        return carry

    lax.fori_loop(0, rows // 128, narrow, 0)
    z_sum = z_sums[z]
    for peer in line_from:
        z_copy(peer, peer).wait_recv()
        z_sum = z_sum + z_in[peer].astype(F32)
    x_part[mine] = z_sum
    for peer in dp_peers:
        x_copy(peer, mine).start()
    for peer in line_from:
        pool_copy(peer, peer).wait_recv()
        own_pool = own_pool + pool_in[peer].astype(F32)
    pooled_ref[...] = own_pool.T.astype(BF16)
    for peer in dp_peers:
        x_copy(peer, peer).wait_recv()
    for d in range(dp):
        lines = slice(d * share, (d + 1) * share)
        change_ref[lines, :] = x_part[d]

    core_copy().wait_send()
    for peer in line_peers:
        code_copy(peer, z).wait_send()
        pool_copy(peer, z).wait_send()
        z_copy(peer, z).wait_send()

    for i in range(PIECES):
        for hop in range(NZ // 2):
            line_copy(0, hop, z, i).wait_send()
        for hop in range(NZ // 2 - 1):
            line_copy(1, hop, z, i).wait_send()

    for k in range(NZ):
        all_g(k).wait_send()
        all_q(k).wait_send()
        all_r(k).wait_send()
    for peer in dp_peers:
        for h in range(HALVES):
            part_copy(peer, mine, h).wait_send()
        x_copy(peer, mine).wait_send()
    for h in range(HALVES):
        for peer in (right, left):
            sum_copy(peer, mine, h).wait_send()
    pass_sum(left, right, 0).wait_send()
    pass_sum(right, left, 1).wait_send()
    for peer in y_peers:
        y_copy(peer, y).wait_send()
    for d in range(dp):
        for h in range(HALVES):
            fresh_copy(d, h).wait()


def publish_kernel(pooled, fresh, accum, change, parity, *outs):
    for one, out in zip((pooled, fresh, accum), outs):
        out[...] = one[...]
    outs[3][...] = parity[...] + change[...]


def on_device(owners, local_rows, grad_pooled, table, accum, parity, parity_slot):
    table_count, dp = lax.axis_size("table"), lax.axis_size("dp")
    bags = owners.shape[0]
    rows, width = table.shape
    index = jnp.arange(table_count, dtype=I32)
    owner_at = (index % NQ // NC * NZ + index // NQ) * NC + index % NC
    named = owners.T[:, None, :] == owner_at[None, :, None]
    hits = jnp.any(named, axis=0)
    wanted = jnp.sum(jnp.where(named, local_rows.T[:, None, :], 0), axis=0)
    before = jnp.arange(bags)[:, None] < jnp.arange(bags)[None, :]
    rank = jnp.dot(hits.astype(BF16), before.astype(BF16), preferred_element_type=F32)
    code = jnp.where(hits, wanted * CAP + rank.astype(I32), -1).reshape(NZ, NQ, bags)

    count = parity.shape[0]
    share = count // dp
    slots = table_count * share
    quarter = rows // dp
    dma = pltpu.SemaphoreType.DMA
    pooled, fresh, new_accum, change = pl.pallas_call(
        step_kernel,
        out_shape=(
            jax.ShapeDtypeStruct((bags, width), BF16),
            jax.ShapeDtypeStruct((rows, width), F32),
            jax.ShapeDtypeStruct((rows // 128, 128), F32),
            jax.ShapeDtypeStruct((count, width), F32),
        ),
        in_specs=[VMEM, VMEM, ANY, VMEM, VMEM],
        out_specs=(VMEM, ANY, VMEM, VMEM),
        scratch_shapes=[
            pltpu.VMEM((rows // 128, 128), I32),
            pltpu.VMEM((rows + 8, width), F32),
            pltpu.VMEM((rows, 128), F32),
            pltpu.VMEM((NZ, bags, width), BF16),
            pltpu.VMEM((NZ, NQ, bags), I32),
            pltpu.VMEM((NZ, NQ * CAP, bags), BF16),
            pltpu.VMEM((NZ, NQ * CAP, width), BF16),
            pltpu.VMEM((NZ, NQ * CAP, width), BF16),
            pltpu.VMEM((NZ, NQ, 1, CAP), I32),
            pltpu.VMEM((NZ, NQ, 1, CAP), I32),
            pltpu.SMEM((NZ, NQ, 1, CAP), I32),
            pltpu.VMEM((NZ, NQ * CAP, width), BF16),
            pltpu.VMEM((NZ, NQ * CAP, width), BF16),
            pltpu.VMEM((quarter, dp * width), F32),
            pltpu.VMEM((dp, quarter, width), BF16),
            pltpu.VMEM((dp, quarter, width), BF16),
            pltpu.VMEM((dp, quarter, width), BF16),
            pltpu.VMEM((NZ, width, bags), BF16),
            pltpu.VMEM((NZ, width, bags), BF16),
            pltpu.VMEM((CAP, width), F32),
            pltpu.VMEM((slots, width), F32),
            pltpu.VMEM((slots // NC, width), BF16),
            pltpu.VMEM((slots // NC, width), BF16),
            pltpu.VMEM((NZ, share, width), BF16),
            pltpu.VMEM((NZ, share, width), BF16),
            pltpu.VMEM((NZ, share, width), F32),
            pltpu.VMEM((NY, NZ * share, width), BF16),
            pltpu.VMEM((NY, NZ * share, width), BF16),
            pltpu.VMEM((dp, share, width), F32),
        ]
        + [dma((NZ,))] * 2
        + [dma((2, NZ // 2, PIECES)), dma((NZ, PIECES))]
        + [dma((NZ,))] * 6
        + [dma((dp, HALVES))] * 4
        + [dma((NZ,))] * 2
        + [dma] * 2
        + [dma((NZ,))] * 2
        + [dma((NY,))] * 2
        + [dma((dp,))] * 2
        + [dma, dma]
        + [pltpu.VMEM((rows, width), F32), dma((dp, HALVES))],
        compiler_params=pltpu.CompilerParams(
            vmem_limit_bytes=56 * 1024 * 1024, collective_id=0, has_side_effects=True
        ),
        name="step",
    )(
        code,
        grad_pooled,
        table,
        accum.reshape(rows // 128, 128),
        parity_slot.reshape(rows // 128, 128),
    )
    def part(array):
        return pl.BlockSpec((array.shape[0] // 4, array.shape[1]), lambda i: (i, 0))

    results = (pooled, fresh, new_accum, change)
    pooled, new_table, new_accum, new_parity = pl.pallas_call(
        publish_kernel,
        grid=(4,),
        out_shape=tuple(jax.ShapeDtypeStruct(one.shape, one.dtype) for one in results),
        in_specs=[part(one) for one in results + (parity,)],
        out_specs=tuple(part(one) for one in results),
        name="publish",
    )(*results, parity)
    return (pooled, new_table, new_accum.reshape(rows), new_parity)


def solution(mesh):
    in_specs = (
        P(("table", "dp"), None),
        P(("table", "dp"), None),
        P(("table", "dp"), None),
        P("table", None),
        P("table"),
        P("table", None),
        P("table"),
    )
    out_specs = (P(("table", "dp"), None), P("table", None), P("table"), P("table", None))
    return jax.shard_map(
        on_device, mesh=mesh, in_specs=in_specs, out_specs=out_specs, check_vma=False
    )
```

```python
import jax
import jax.numpy as jnp
from jax import lax
from jax.experimental import pallas as pl
from jax.experimental.pallas import tpu as pltpu
from jax.sharding import PartitionSpec as P

LEARN = 0.5
EPSILON = 1e-06
F32, BF16, I32 = jnp.float32, jnp.bfloat16, jnp.int32
ANY = pl.BlockSpec(memory_space=pl.ANY)
VMEM = pl.BlockSpec(memory_space=pltpu.VMEM)
MESH = pl.DeviceIdType.MESH
NY, NZ, NC = 4, 8, 2
NQ = NY * NC
CAP = 128
HALVES = 2
PIECES = 2


def near(k):
    j = (k + 1) // 2
    return (k % 2) * j + (1 - k % 2) * ((NZ - j) % NZ)


def step_kernel(
    code_ref, grads_ref, table_ref, accum_ref, home_ref,
    pooled_ref, fresh_ref, new_accum_ref, change_ref,
    slot_ref, table, wide_accum, line_in, code_in, marks, g_out, g_in, q_out, q_in, q_smem, r_out, r_in,
    total, part, quarter_in, sums, pool_out, pool_in, line, placed, core_out, core_in,
    z_out, z_in, z_sums, y_out, y_in, x_part,
    code_s, code_r, line_s, line_r, g_s, g_r, q_s, q_r, r_s, r_r, part_s, part_r, sum_s, sum_r,
    pool_s, pool_r, core_s, core_r, z_s, z_r, y_s, y_r, x_s, x_r, table_sem, smem_sem, fresh, fresh_sem,
):
    bags = code_ref.shape[2]
    rows, width = table_ref.shape
    dp = sums.shape[0]
    quarter = rows // dp
    half = quarter // HALVES
    me, mine = lax.axis_index("table"), lax.axis_index("dp")
    z, c, y = (me // NC) % NZ, me % NC, me // (NC * NZ)
    q = y * NC + c

    def remote(src, dst, send, recv, **where):
        return pltpu.make_async_remote_copy(
            src_ref=src, dst_ref=dst, send_sem=send, recv_sem=recv, device_id=where,
            device_id_type=MESH,
        )

    def on_line(other):
        return (me - z * NC) + other * NC

    def on_plane(other):
        return (other // NC) * (NZ * NC) + z * NC + other % NC

    def code_copy(peer, place):
        return remote(code_ref.at[peer], code_in.at[place], code_s.at[peer], code_r.at[place],
                      table=on_line(peer))

    piece = bags // PIECES

    def line_copy(way, hop, origin, i):
        block = line_in.at[origin, pl.ds(i * piece, piece)]
        return remote(block, block, line_s.at[way, hop, i], line_r.at[origin, i],
                      table=on_line((z + 1 + way * (NZ - 2)) % NZ))

    def r_rows(o):
        return pl.ds(pl.multiple_of(o * CAP, CAP), CAP)

    def g_copy(peer, place, s):
        return remote(g_out.at[s, r_rows(peer)], g_in.at[s, r_rows(place)], g_s.at[s],
                      g_r.at[s], table=on_plane(peer))

    def q_copy(peer, place, s):
        return remote(q_out.at[s, peer], q_in.at[s, place], q_s.at[s], q_r.at[s],
                      table=on_plane(peer))

    def r_copy(peer, place, s):
        return remote(r_out.at[s, r_rows(peer)], r_in.at[s, r_rows(place)], r_s.at[s],
                      r_r.at[s], table=on_plane(peer))

    others = pl.ds(0, NQ - 1)
    other_rows = pl.ds(0, (NQ - 1) * CAP)

    def all_g(s):
        return remote(g_out.at[s, other_rows], g_in.at[s, other_rows], g_s.at[s], g_r.at[s],
                      table=on_plane((q + 1) % NQ))

    def all_q(s):
        return remote(q_out.at[s, others], q_in.at[s, others], q_s.at[s], q_r.at[s],
                      table=on_plane((q + 1) % NQ))

    def all_r(s):
        return remote(r_out.at[s, other_rows], r_in.at[s, other_rows], r_s.at[s], r_r.at[s],
                      table=on_plane((q + 1) % NQ))

    def half_rows(h):
        return pl.ds(h * half, half)

    def part_copy(peer, place, h):
        return remote(part.at[peer, half_rows(h)], quarter_in.at[place, half_rows(h)],
                      part_s.at[peer, h], part_r.at[place, h], dp=peer)

    def sum_copy(peer, place, h):
        return remote(sums.at[place, half_rows(h)], sums.at[place, half_rows(h)],
                      sum_s.at[peer, h], sum_r.at[place, h], dp=peer)

    def pool_copy(peer, place):
        return remote(pool_out.at[peer], pool_in.at[place], pool_s.at[peer], pool_r.at[place],
                      table=on_line(peer))

    def core_copy():
        return remote(core_out, core_in, core_s, core_r, table=me + 1 - 2 * c)

    def z_copy(peer, place):
        return remote(z_out.at[peer], z_in.at[place], z_s.at[peer], z_r.at[place],
                      table=on_line(peer))

    def y_copy(peer, place):
        return remote(y_out.at[peer], y_in.at[place], y_s.at[peer], y_r.at[place],
                      table=on_plane(peer * NC + c))

    def x_copy(peer, place):
        return remote(x_part.at[place], x_part.at[place], x_s.at[peer], x_r.at[place], dp=peer)

    line_peers = [(z + near(k)) % NZ for k in range(1, NZ)]
    line_from = [(z + NZ - near(k)) % NZ for k in range(1, NZ)]
    plane_peers = [(q + k) % NQ for k in range(1, NQ)]
    dp_peers = [(mine + k) % dp for k in (1, 3, 2)]
    right, left, far = [(mine + k) % dp for k in (1, dp - 1, 2)]
    y_peers = [(y + k) % NY for k in (1, 3, 2)]

    load = pltpu.make_async_copy(table_ref, table.at[0:rows], table_sem)
    load.start()
    barrier = pltpu.get_barrier_semaphore()
    for peer in line_peers:
        pl.semaphore_signal(barrier, inc=1, device_id={"table": on_line(peer)}, device_id_type=MESH)
    for peer in plane_peers:
        pl.semaphore_signal(barrier, inc=1, device_id={"table": on_plane(peer)}, device_id_type=MESH)
    for peer in dp_peers:
        pl.semaphore_signal(barrier, inc=1, device_id={"dp": peer}, device_id_type=MESH)

    pl.semaphore_wait(barrier, len(line_peers) + len(plane_peers) + len(dp_peers))
    line_in[z] = grads_ref[...]
    for i in range(PIECES):
        for way in (0, 1):
            line_copy(way, 0, z, i).start()
    for peer in line_peers:
        code_copy(peer, z).start()
    code_in[z] = code_ref[z]

    slot = lax.broadcasted_iota(I32, (CAP, bags), 0)

    def pack(i):
        s = (z + NZ - near(i)) % NZ

        @pl.when(i > 0)
        def _():
            code_copy(s, s).wait_recv()

        for o in range(NQ):
            code = code_in[s, o : o + 1, :]
            hot = slot == jnp.where(code < 0, -1, code & (CAP - 1))
            marks[s, o * CAP : (o + 1) * CAP, :] = hot.astype(F32).astype(BF16)
            named = jnp.where(hot, (code >> 7) + 1, 0)
            named = sum(named[:, b : b + CAP] for b in range(0, bags, CAP))
            named = jnp.sum(named.T, axis=0, keepdims=True)
            q_out[s, o] = jnp.where(named == 0, rows, named - 1)
        for peer in plane_peers:
            q_copy(peer, q, s).start()
        q_in[s, q] = q_out[s, q]
        g_out[s] = jnp.dot(marks[s], line_in[s], preferred_element_type=F32).astype(BF16)
        for peer in plane_peers:
            g_copy(peer, q, s).start()
        g_in[s, r_rows(q), :] = g_out[s, r_rows(q), :]

    def pass_on(h):
        for i in range(PIECES):
            for way, last in ((0, NZ // 2), (1, NZ // 2 - 1)):
                origin = (z + NZ - h + way * 2 * h) % NZ

                @pl.when(h <= last)
                def _():
                    line_copy(way, 0, origin, i).wait_recv()

                @pl.when(h < last)
                def _():
                    line_copy(way, h, origin, i).start()

    chunk = 256
    low_row = lax.broadcasted_iota(I32, (chunk, CAP), 0)

    def add(i):
        s = (z + NZ - near(i)) % NZ
        all_q(s).wait_recv()
        all_g(s).wait_recv()
        names = [q_in[s, o] for o in range(NQ)]
        high = (jnp.concatenate(names, axis=0) // quarter).T
        grads = []
        for o in range(NQ):
            block = jnp.broadcast_to(high[:, o : o + 1], (CAP, width))
            lines = g_in[s, o * CAP : (o + 1) * CAP, :]
            grads.append(
                jnp.concatenate([(block == d).astype(F32).astype(BF16) * lines for d in range(dp)], axis=1)
            )
        grads = jnp.concatenate(grads, axis=0)
        low = [one & (quarter - 1) for one in names]
        for b in range(0, quarter, chunk):
            hot = jnp.concatenate(
                [(low_row == one - b).astype(F32).astype(BF16) for one in low], axis=1
            )
            total[b : b + chunk, :] += jnp.dot(hot, grads, preferred_element_type=F32)

    share = change_ref.shape[0] // dp

    def prepare():
        count = change_ref.shape[0]
        home = home_ref[...]
        holder, place = home // count, home % count
        order = (holder % NC * NY + holder // (NZ * NC)) * NZ + holder // NC % NZ
        slot_ref[...] = jnp.where(place // share == mine, order * share + place % share, -1)

        table[rows : rows + 8, :] = jnp.zeros((8, width), F32)
        total[...] = jnp.zeros_like(total)
        placed[...] = jnp.zeros_like(placed)

        def widen(i, carry):
            block = jnp.broadcast_to(accum_ref[pl.ds(i, 1), :], (128, 128))
            wide_accum[pl.ds(pl.multiple_of(i * 128, 128), 128), :] = block.T
            return carry

        lax.fori_loop(0, rows // 128, widen, 0)

    def relay(p, carry):
        def packs(i, carry):
            pl.when(jnp.logical_and(i >= 0, i < NZ))(lambda: pack(i))
            return carry

        def adds(i, carry):
            add(i)
            return carry

        lax.fori_loop(2 * p - 1, 2 * p + 1, packs, 0)
        pl.when(p == 0)(prepare)
        pass_on(p + 1)
        lax.fori_loop(jnp.maximum(2 * p - 3, 0), jnp.maximum(2 * p - 1, 0), adds, 0)
        return carry

    lax.fori_loop(0, NZ // 2 + 1, relay, 0)
    lax.fori_loop(NZ - 1, NZ, lambda i, carry: (add(i), carry)[1], 0)
    def part_start(h):
        for d in range(dp):
            part[d, half_rows(h), :] = total[half_rows(h), d * width : (d + 1) * width].astype(BF16)
        for peer in dp_peers:
            part_copy(peer, mine, h).start()

    part_start(0)

    fetch = pltpu.make_async_copy(q_in, q_smem, smem_sem)
    fetch.start()
    fetch.wait()
    load.wait()

    def pick(o, s):
        for i in range(CAP):
            line[pl.ds(i, 1), :] = table[pl.ds(q_smem[s, o, 0, i], 1), :]
        return line[...].astype(BF16)

    def serve(j):
        s = (z + near(NZ - 1 - j)) % NZ

        def one(k, carry):
            o = (q + k) % NQ
            r_out[s, r_rows(o), :] = pick(o, s)
            r_copy(o, q, s).start()
            return carry

        lax.fori_loop(1, NQ, one, 0)
        r_in[s, r_rows(q), :] = pick(q, s)

    def pool(i, carry):
        s = (z + near(NZ - 1 - i)) % NZ
        all_r(s).wait_recv()
        pooled = lax.dot_general(
            r_in[s], marks[s], (((0,), (0,)), ((), ())), preferred_element_type=F32
        )
        pool_out[s] = pooled.astype(BF16)
        pool_copy(s, z).start()
        return carry


    def dp_sum(h):
        summed = part[mine, half_rows(h), :].astype(F32)
        for peer in dp_peers:
            part_copy(peer, peer, h).wait_recv()
            summed = summed + quarter_in[peer, half_rows(h), :].astype(F32)
        sums[mine, half_rows(h), :] = summed.astype(BF16)
        for peer in (right, left):
            sum_copy(peer, mine, h).start()

    def serves(j, carry):
        serve(j)

        @pl.when(j >= 4)
        def _():
            pool(j - 4, 0)

        return carry

    lax.fori_loop(0, 4, serves, 0)
    part_start(1)
    lax.fori_loop(4, 5, serves, 0)
    dp_sum(0)
    lax.fori_loop(5, NZ, serves, 0)
    dp_sum(1)

    slots = placed.shape[0]
    place_chunk = 256
    place_row = lax.broadcasted_iota(I32, (place_chunk, 128), 0)

    def fresh_copy(d, h):
        there = pl.ds(pl.multiple_of(d * quarter + h * half, half), half)
        return pltpu.make_async_copy(fresh.at[there], fresh_ref.at[there], fresh_sem.at[d, h])

    def update(d, h):
        base = pl.multiple_of(d * quarter + h * half, half)
        there = pl.ds(base, half)
        g = sums[d, half_rows(h), :].astype(F32)
        squares = jnp.sum(g * g, axis=1, keepdims=True) * (1.0 / width)
        accum = wide_accum[there, :] + squares
        wide_accum[there, :] = accum
        delta = g * (-LEARN) * lax.rsqrt(accum + EPSILON)
        fresh[there, :] = table[there, :] + delta
        fresh_copy(d, h).start()
        delta = delta.astype(BF16)
        lines = [slot_ref[pl.ds(base // 128 + i, 1), :] for i in range(half // 128)]
        for b in range(0, slots, place_chunk):
            hot = jnp.concatenate(
                [(place_row == one - b).astype(F32).astype(BF16) for one in lines], axis=1
            )
            placed[b : b + place_chunk, :] += jnp.dot(hot, delta, preferred_element_type=F32)

    def pass_sum(origin, peer, h):
        block = sums.at[origin, half_rows(h)]
        return remote(block, block, sum_s.at[far, h], sum_r.at[origin, h], dp=peer)

    def arrived(d, h):
        sum_copy(d, d, h).wait_recv()
        if d is left and h == 0:
            pass_sum(left, right, 0).start()
        if d is right and h == 1:
            pass_sum(right, left, 1).start()
        update(d, h)

    update(mine, 0)
    arrived(left, 0)
    arrived(right, 0)
    update(mine, 1)
    arrived(right, 1)
    arrived(left, 1)
    lax.fori_loop(4, 6, pool, 0)
    arrived(far, 0)
    arrived(far, 1)

    per_core = slots // NC
    core_out[...] = placed[pl.ds(pl.multiple_of((1 - c) * per_core, per_core), per_core), :].astype(BF16)
    core_copy().start()
    kept = pl.ds(pl.multiple_of(c * per_core, per_core), per_core)
    core_copy().wait_recv()
    placed[kept, :] = placed[kept, :] + core_in[...].astype(F32)
    per_y = per_core // NY
    for peer in y_peers:
        begin = pl.multiple_of(c * per_core + peer * per_y, per_y)
        y_out[peer] = placed[pl.ds(begin, per_y), :].astype(BF16)
        y_copy(peer, y).start()
    y_sum = placed[pl.ds(pl.multiple_of(c * per_core + y * per_y, per_y), per_y), :]
    lax.fori_loop(6, NZ - 1, pool, 0)
    for peer in y_peers:
        y_copy(peer, peer).wait_recv()
        y_sum = y_sum + y_in[peer].astype(F32)
    for k in range(NZ):
        z_sums[k] = y_sum[k * share : (k + 1) * share, :]
    for peer in line_peers:
        z_out[peer] = z_sums[peer].astype(BF16)
        z_copy(peer, z).start()
    all_r(z).wait_recv()
    own_pool = lax.dot_general(
        r_in[z], marks[z], (((0,), (0,)), ((), ())), preferred_element_type=F32
    )

    def narrow(i, carry):
        block = wide_accum[pl.ds(pl.multiple_of(i * 128, 128), 128), :]
        new_accum_ref[pl.ds(i, 1), :] = block.T[0:1, :]
        return carry

    lax.fori_loop(0, rows // 128, narrow, 0)
    z_sum = z_sums[z]
    for peer in line_from:
        z_copy(peer, peer).wait_recv()
        z_sum = z_sum + z_in[peer].astype(F32)
    x_part[mine] = z_sum
    for peer in dp_peers:
        x_copy(peer, mine).start()
    for peer in line_from:
        pool_copy(peer, peer).wait_recv()
        own_pool = own_pool + pool_in[peer].astype(F32)
    pooled_ref[...] = own_pool.T.astype(BF16)
    for peer in dp_peers:
        x_copy(peer, peer).wait_recv()
    for d in range(dp):
        lines = slice(d * share, (d + 1) * share)
        change_ref[lines, :] = x_part[d]

    core_copy().wait_send()
    for peer in line_peers:
        code_copy(peer, z).wait_send()
        pool_copy(peer, z).wait_send()
        z_copy(peer, z).wait_send()

    for i in range(PIECES):
        for hop in range(NZ // 2):
            line_copy(0, hop, z, i).wait_send()
        for hop in range(NZ // 2 - 1):
            line_copy(1, hop, z, i).wait_send()

    for k in range(NZ):
        all_g(k).wait_send()
        all_q(k).wait_send()
        all_r(k).wait_send()
    for peer in dp_peers:
        for h in range(HALVES):
            part_copy(peer, mine, h).wait_send()
        x_copy(peer, mine).wait_send()
    for h in range(HALVES):
        for peer in (right, left):
            sum_copy(peer, mine, h).wait_send()
    pass_sum(left, right, 0).wait_send()
    pass_sum(right, left, 1).wait_send()
    for peer in y_peers:
        y_copy(peer, y).wait_send()
    for d in range(dp):
        for h in range(HALVES):
            fresh_copy(d, h).wait()


def publish_kernel(pooled, fresh, accum, change, parity, *outs):
    for one, out in zip((pooled, fresh, accum), outs):
        out[...] = one[...]
    outs[3][...] = parity[...] + change[...]


def on_device(owners, local_rows, grad_pooled, table, accum, parity, parity_slot):
    table_count, dp = lax.axis_size("table"), lax.axis_size("dp")
    bags = owners.shape[0]
    rows, width = table.shape
    index = jnp.arange(table_count, dtype=I32)
    owner_at = (index % NQ // NC * NZ + index // NQ) * NC + index % NC
    named = owners.T[:, None, :] == owner_at[None, :, None]
    wanted = jnp.sum(jnp.where(named, local_rows.T[:, None, :] + 1, 0), axis=0)
    hits = wanted > 0
    before = jnp.arange(bags)[:, None] < jnp.arange(bags)[None, :]
    rank = jnp.dot(hits.astype(BF16), before.astype(BF16), preferred_element_type=F32)
    code = jnp.where(hits, (wanted - 1) * CAP + rank.astype(I32), -1).reshape(NZ, NQ, bags)

    count = parity.shape[0]
    share = count // dp
    slots = table_count * share
    quarter = rows // dp
    dma = pltpu.SemaphoreType.DMA
    pooled, fresh, new_accum, change = pl.pallas_call(
        step_kernel,
        out_shape=(
            jax.ShapeDtypeStruct((bags, width), BF16),
            jax.ShapeDtypeStruct((rows, width), F32),
            jax.ShapeDtypeStruct((rows // 128, 128), F32),
            jax.ShapeDtypeStruct((count, width), F32),
        ),
        in_specs=[VMEM, VMEM, ANY, VMEM, VMEM],
        out_specs=(VMEM, ANY, VMEM, VMEM),
        scratch_shapes=[
            pltpu.VMEM((rows // 128, 128), I32),
            pltpu.VMEM((rows + 8, width), F32),
            pltpu.VMEM((rows, 128), F32),
            pltpu.VMEM((NZ, bags, width), BF16),
            pltpu.VMEM((NZ, NQ, bags), I32),
            pltpu.VMEM((NZ, NQ * CAP, bags), BF16),
            pltpu.VMEM((NZ, NQ * CAP, width), BF16),
            pltpu.VMEM((NZ, NQ * CAP, width), BF16),
            pltpu.VMEM((NZ, NQ, 1, CAP), I32),
            pltpu.VMEM((NZ, NQ, 1, CAP), I32),
            pltpu.SMEM((NZ, NQ, 1, CAP), I32),
            pltpu.VMEM((NZ, NQ * CAP, width), BF16),
            pltpu.VMEM((NZ, NQ * CAP, width), BF16),
            pltpu.VMEM((quarter, dp * width), F32),
            pltpu.VMEM((dp, quarter, width), BF16),
            pltpu.VMEM((dp, quarter, width), BF16),
            pltpu.VMEM((dp, quarter, width), BF16),
            pltpu.VMEM((NZ, width, bags), BF16),
            pltpu.VMEM((NZ, width, bags), BF16),
            pltpu.VMEM((CAP, width), F32),
            pltpu.VMEM((slots, width), F32),
            pltpu.VMEM((slots // NC, width), BF16),
            pltpu.VMEM((slots // NC, width), BF16),
            pltpu.VMEM((NZ, share, width), BF16),
            pltpu.VMEM((NZ, share, width), BF16),
            pltpu.VMEM((NZ, share, width), F32),
            pltpu.VMEM((NY, NZ * share, width), BF16),
            pltpu.VMEM((NY, NZ * share, width), BF16),
            pltpu.VMEM((dp, share, width), F32),
        ]
        + [dma((NZ,))] * 2
        + [dma((2, NZ // 2, PIECES)), dma((NZ, PIECES))]
        + [dma((NZ,))] * 6
        + [dma((dp, HALVES))] * 4
        + [dma((NZ,))] * 2
        + [dma] * 2
        + [dma((NZ,))] * 2
        + [dma((NY,))] * 2
        + [dma((dp,))] * 2
        + [dma, dma]
        + [pltpu.VMEM((rows, width), F32), dma((dp, HALVES))],
        compiler_params=pltpu.CompilerParams(
            vmem_limit_bytes=56 * 1024 * 1024, collective_id=0, has_side_effects=True
        ),
        name="step",
    )(
        code,
        grad_pooled,
        table,
        accum.reshape(rows // 128, 128),
        parity_slot.reshape(rows // 128, 128),
    )
    def part(array):
        return pl.BlockSpec((array.shape[0] // 4, array.shape[1]), lambda i: (i, 0))

    results = (pooled, fresh, new_accum, change)
    pooled, new_table, new_accum, new_parity = pl.pallas_call(
        publish_kernel,
        grid=(4,),
        out_shape=tuple(jax.ShapeDtypeStruct(one.shape, one.dtype) for one in results),
        in_specs=[part(one) for one in results + (parity,)],
        out_specs=tuple(part(one) for one in results),
        name="publish",
    )(*results, parity)
    return (pooled, new_table, new_accum.reshape(rows), new_parity)


def solution(mesh):
    in_specs = (
        P(("table", "dp"), None),
        P(("table", "dp"), None),
        P(("table", "dp"), None),
        P("table", None),
        P("table"),
        P("table", None),
        P("table"),
    )
    out_specs = (P(("table", "dp"), None), P("table", None), P("table"), P("table", None))
    return jax.shard_map(
        on_device, mesh=mesh, in_specs=in_specs, out_specs=out_specs, check_vma=False
    )
```
